32 devices in a mesh: los: 32 (over z, y, x, core), sky: 1.
Axes of the slice: x: 2, y: 2, z: 4, core: 2. Of those that a mesh axis runs over, the one named last changes fastest.
Arguments:
- part_cell: int32 [3, 131072], P(None, ('los', 'sky')), may hold values from 0 to 127, as said below
- part_frac: float32 [3, 131072], P(None, ('los', 'sky')), may hold values from 0 to 1
- los_offset: int32 [131072], P(('los', 'sky')), may hold values from -32 to 32
- block_dest: int32 [1024], P(('los', 'sky')), may hold values from 0 to 31, as said below
- block_count: int32 [1024], P(('los', 'sky')), may hold values from 96 to 128, as said below
- selection: float32 [128, 4, 128], P('los', 'sky'), may hold values from 0.3 to 3
- galaxy_counts: int32 [128, 4, 128], P('los', 'sky'), may hold values from 0 to 5
- bias_exp: float32 [128], P('los'), may hold values from 1.2 to 2.2
- rsd_factor: float32 [128], P('los'), may hold values from 0.5 to 2
Outputs:
- grad_pos: float32 [3, 131072], P(None, ('los', 'sky'))
- grad_vel: float32 [131072], P(('los', 'sky'))
The draws below stay inside these ranges and needn't reach their ends.
Inputs may be any that keep to these rules, and one draw needn't show every extreme that they name: Component 1 of a particle lies in the first-sky cells of its own device's columns, and (part_cell[0] + los_offset) mod 128 lies in cells block_dest * 4 to block_dest * 4 + 3 of the particle's block, for every slot. `block_dest`: the 32 blocks of one device name any slab at most 2 times, and on every device some slab is named exactly 2 times. `block_count`: A block's live particles are its first slots; every device has a full block.
All inputs are finite; a program needn't handle non-finite values.
Results may differ from the reference program's by a relative error of at most 0.000098.
Values sent between devices are 32-bit elements; how exact they have to be, the bound alone decides.
No kernel may reach another device: no remote copies, remote signals or barrier semaphores. Data moves between devices by JAX's collectives and lax.ppermute only.
A program may use at most 64 MiB of HBM per device.

```python
import math
import jax
import jax.numpy as jnp
from jax import lax

CL = 4
CA = 4
NB = 128
NBK = 32
BLK = 128
MAXOFF = 32
PART = 131072
NL = 128
NA = 4
N_LOS = 32
N_SKY = 1


def routing(key):
    subkeys = jax.random.split(jax.random.fold_in(key, 11), 10)
    devices = N_LOS * N_SKY
    capacity = 2 * NBK // N_LOS
    slot_count = N_LOS * capacity
    slot_dest = jnp.arange(slot_count, dtype=jnp.int32) // capacity
    favour = jax.random.randint(subkeys[0], (N_LOS,), 0, 2048)
    hottest = jax.random.randint(subkeys[1], (devices,), 0, N_LOS)
    jitter = jax.random.randint(subkeys[2], (devices, slot_count), 0, 1024)
    scores = favour[slot_dest][None, :] + jitter + jnp.where(slot_dest[None, :] == hottest[:, None], 4096, 0)
    scores = scores * slot_count + jnp.arange(slot_count, dtype=jnp.int32)[None, :]
    top_scores, chosen = lax.top_k(scores, NBK)
    shuffle = jax.random.randint(subkeys[3], (devices, NBK), 0, 1 << 20) * NBK + jnp.arange(NBK, dtype=jnp.int32)[None, :]
    reorder = jnp.argsort(shuffle, axis=1)
    chosen = jnp.take_along_axis(chosen, reorder, axis=1)
    target_slab = (chosen // capacity).astype(jnp.int32)
    counts = jax.random.randint(subkeys[4], (devices, NBK), max(1, 3 * BLK // 4), BLK + 1)
    full_at = jax.random.randint(subkeys[5], (devices,), 0, NBK)
    counts = jnp.where(jnp.arange(NBK, dtype=jnp.int32)[None, :] == full_at[:, None], BLK, counts)
    grid_shape = (devices, NBK, BLK)
    red_cell = target_slab[:, :, None] * CL + jax.random.randint(subkeys[6], grid_shape, 0, CL)
    offset = jax.random.randint(subkeys[7], grid_shape, -MAXOFF, MAXOFF + 1)
    los_cell = jnp.mod(red_cell - offset, CL * N_LOS)
    sky_index = jnp.arange(devices, dtype=jnp.int32) % N_SKY
    sky_cell = sky_index[:, None, None] * CA + jax.random.randint(subkeys[8], grid_shape, 0, CA)
    deep_cell = jax.random.randint(subkeys[9], grid_shape, 0, NB)
    cells = jnp.stack([los_cell, sky_cell, deep_cell]).reshape(3, -1).astype(jnp.int32)
    return (cells, offset.reshape(-1).astype(jnp.int32), target_slab.reshape(-1), counts.reshape(-1).astype(jnp.int32))


def draw_part_cell(key, part):
    return routing(key)[0]


def draw_los_offset(key, part):
    return routing(key)[1]


def draw_block_dest(key, part):
    return routing(key)[2]


def draw_block_count(key, part):
    return routing(key)[3]


def set_ends(array, key, low, largest):
    longest = array.shape.index(max(array.shape))
    spots = []
    for shift in (0, 1):
        where = [jax.random.randint(jax.random.fold_in(key, axis), (), 0, length) for axis, length in enumerate(array.shape)]
        where[longest] = (where[longest] + shift) % array.shape[longest]
        spots.append(tuple(where))
    return array.at[spots[0]].set(low).at[spots[1]].set(largest)


def block_levels(rng, shape, shards, least, high):
    def one(axis_at, parts):
        steps = jax.random.uniform(jax.random.fold_in(jax.random.fold_in(rng, 6), axis_at), (parts,), jnp.float32, least / len(shards), high / len(shards))
        return jnp.repeat(jnp.exp(steps), shape[axis_at] // parts).reshape((-1,) + (1,) * (len(shape) - axis_at - 1))

    level = one(*shards[0])
    for cut in shards[1:]:
        level = level * one(*cut)
    return level


def setup_inputs(seed: int = 0) -> dict:
    arg_keys = jax.random.split(jax.random.key(seed), 10)
    part_cell = draw_part_cell(jax.random.fold_in(arg_keys[9], 71), 0)
    part_frac = jnp.clip(1.0 * jax.random.uniform(arg_keys[1], (3, PART), jnp.float32) ** block_levels(arg_keys[1], (3, PART), ((1, 32),), -0.2, 0.2), 0.0, 1.0)
    los_offset = draw_los_offset(jax.random.fold_in(arg_keys[9], 71), 0)
    block_dest = draw_block_dest(jax.random.fold_in(arg_keys[9], 71), 0)
    block_count = draw_block_count(jax.random.fold_in(arg_keys[9], 71), 0)
    selection = jnp.clip(jnp.exp(math.log(3.0) - 2.3025851 * jax.random.uniform(arg_keys[5], (NL, NA, NB), jnp.float32) ** block_levels(arg_keys[5], (NL, NA, NB), ((0, 32),), -0.2, 0.2)), 0.3, 3.0)
    galaxy_counts = set_ends(jax.random.randint(arg_keys[6], (NL, NA, NB), 0, 6), jax.random.fold_in(arg_keys[6], 1), 0, 5).astype(jnp.int32)
    bias_exp = jnp.clip(jnp.exp(math.log(2.2) - 0.6061358 * jax.random.uniform(arg_keys[7], (NL,), jnp.float32) ** block_levels(arg_keys[7], (NL,), ((0, 32),), -0.2, 0.2)), 1.2, 2.2)
    rsd_factor = jnp.clip(jnp.exp(math.log(2.0) - 1.3862944 * jax.random.uniform(arg_keys[8], (NL,), jnp.float32) ** block_levels(arg_keys[8], (NL,), ((0, 32),), -0.2, 0.2)), 0.5, 2.0)
    return dict(part_cell=part_cell, part_frac=part_frac, los_offset=los_offset, block_dest=block_dest, block_count=block_count, selection=selection, galaxy_counts=galaxy_counts, bias_exp=bias_exp, rsd_factor=rsd_factor)


def corner_bits():
    return [(los_bit, sky_bit, deep_bit) for los_bit in (0, 1) for sky_bit in (0, 1) for deep_bit in (0, 1)]


def factor(fraction, bit):
    return fraction if bit else 1.0 - fraction


def slope(bit):
    return 1.0 if bit else -1.0


def reference(part_cell, part_frac, los_offset, block_dest, block_count, selection, galaxy_counts, bias_exp, rsd_factor):
    slot_index = jnp.arange(BLK, dtype=jnp.int32)
    alive = (slot_index[None, :] < block_count[:, None]).astype(jnp.float32).reshape(-1)
    dest_each = jnp.repeat(block_dest, BLK).astype(jnp.int32)
    red_cell = (dest_each * CL + jnp.mod(part_cell[0] + los_offset, CL)).astype(jnp.int32)
    sky_cell = part_cell[1]
    deep_cell = part_cell[2]
    frac_los = part_frac[0]
    frac_sky = part_frac[1]
    frac_deep = part_frac[2]
    density = jnp.zeros((NL * NA * NB,), jnp.float32)
    flat_list = []
    slope_list = []
    for bits in corner_bits():
        flat_index = ((jnp.mod(red_cell + bits[0], NL) * NA + jnp.mod(sky_cell + bits[1], NA)) * NB + jnp.mod(deep_cell + bits[2], NB)).astype(jnp.int32)
        weight_los = factor(frac_los, bits[0])
        weight_sky = factor(frac_sky, bits[1])
        weight_deep = factor(frac_deep, bits[2])
        weight = weight_los * weight_sky * weight_deep
        density = density.at[flat_index].add(weight * alive)
        flat_list.append(flat_index)
        slope_list.append((slope(bits[0]) * weight_sky * weight_deep, weight_los * slope(bits[1]) * weight_deep, weight_los * weight_sky * slope(bits[2])))
    density = density.reshape(NL, NA, NB)
    shifted = density + 0.5
    exponent = bias_exp[:, None, None]
    intensity = selection * jnp.exp(exponent * jnp.log(shifted))
    cotangent = (1.0 - galaxy_counts.astype(jnp.float32) / intensity) * exponent * intensity / shifted
    flat_field = cotangent.reshape(-1)
    grad_los = jnp.zeros((PART,), jnp.float32)
    grad_sky = jnp.zeros((PART,), jnp.float32)
    grad_deep = jnp.zeros((PART,), jnp.float32)
    for flat_index, slopes in zip(flat_list, slope_list):
        picked = flat_field[flat_index]
        grad_los = grad_los + slopes[0] * picked
        grad_sky = grad_sky + slopes[1] * picked
        grad_deep = grad_deep + slopes[2] * picked
    grad_pos = jnp.stack([grad_los, grad_sky, grad_deep]) * alive[None, :]
    grad_vel = rsd_factor[red_cell] * grad_los * alive
    return grad_pos, grad_vel
```

```python
import functools

import jax
import jax.numpy as jnp
from jax import lax
from jax.experimental import pallas as pl
from jax.experimental.pallas import tpu as pltpu
from jax.sharding import PartitionSpec as P

SUB = 8


def passed_along(block, axis, distance):
    devices = range(lax.axis_size(axis))
    route = [((i - distance) % len(devices), i) for i in devices]
    return lax.ppermute(block, axis, route)


def exchanged(chunks):
    return lax.all_to_all(chunks, "los", split_axis=0, concat_axis=0, tiled=True)


def rounded_up(value, step):
    return -(-value // step) * step


def row_iotas(cols):
    sub = lax.broadcasted_iota(jnp.int32, (SUB, 128), 0)
    return sub // cols, sub % cols


def block_rows(ref, row, k, lanes):
    return jnp.broadcast_to(ref[row : row + 1, k * lanes : (k + 1) * lanes], (SUB, lanes))


def paint_kernel(
    g, dest_ref, count_ref, cell_ref, frac_ref, offset_ref, out_ref, low_ref, high_ref
):
    low_ref[...] = jnp.zeros_like(low_ref)
    high_ref[...] = jnp.zeros_like(high_ref)
    plane_iota, sky_iota = row_iotas(g.cols)
    deep_iota = lax.broadcasted_iota(jnp.int32, (g.deep, g.block), 0)
    lane = lax.broadcasted_iota(jnp.int32, (SUB, g.block), 1)
    for k in range(g.blocks):
        offset = jnp.broadcast_to(offset_ref[k : k + 1, :], (SUB, g.block))
        red = jnp.mod(block_rows(cell_ref, 0, k, g.block) + offset, g.slab_rows)
        sky = block_rows(cell_ref, 1, k, g.block)
        sky_next = jnp.where(sky + 1 == g.sky_wrap, 0, sky + 1)
        frac_los = block_rows(frac_ref, 0, k, g.block)
        frac_sky = block_rows(frac_ref, 1, k, g.block)
        frac_deep = block_rows(frac_ref, 2, k, g.block)
        live = lane < count_ref[k]
        on_sky = jnp.where(
            sky_iota == sky, 1.0 - frac_sky, jnp.where(sky_iota == sky_next, frac_sky, 0.0)
        )
        on_sky = jnp.where(live, on_sky, 0.0)
        rows = []
        for i in range(g.window // SUB):
            plane = plane_iota + i * g.planes_per_tile - red
            on_los = jnp.where(
                plane == 0, 1.0 - frac_los, jnp.where(plane == 1, frac_los, 0.0)
            )
            rows.append(on_los * on_sky)
        weight = jnp.concatenate(rows, axis=0)
        upper = weight * jnp.concatenate([frac_deep] * (g.window // SUB), axis=0)
        weight = jnp.concatenate([weight - upper, upper], axis=0)
        coarse = weight.astype(jnp.bfloat16)
        fine = (weight - coarse.astype(jnp.float32)).astype(jnp.bfloat16)
        deep = jnp.broadcast_to(cell_ref[2:3, k * g.block : (k + 1) * g.block], (g.deep, g.block))
        hit = jnp.where(deep_iota == deep, 1.0, 0.0).astype(jnp.bfloat16)
        got = lax.dot_general(
            jnp.concatenate([coarse, fine], axis=0),
            hit,
            (((1,), (1,)), ((), ())),
            preferred_element_type=jnp.float32,
        )
        got = got[: 2 * g.window] + got[2 * g.window :]
        at = pl.ds(pl.multiple_of(dest_ref[k] * g.slab, SUB), g.window)
        low_ref[at, :] += got[: g.window]
        high_ref[at, :] += got[g.window :]
    total = low_ref[...] + pltpu.roll(high_ref[...], 1, 1)
    size = g.slabs * g.slab
    spill = g.window - g.slab
    out_ref[spill:, :] = total[spill:size]
    out_ref[:spill, :] = total[:spill] + total[size:]


def cotangent_of(density, selection, counts, exponent):
    shifted = density + 0.5
    intensity = selection * jnp.exp(exponent * jnp.log(shifted))
    return (1.0 - counts.astype(jnp.float32) / intensity) * exponent * intensity / shifted


def field_kernel(g, recv_ref, selection_ref, counts_ref, bias_ref, rate_ref, out_ref):
    density = recv_ref[0]
    for i in range(1, g.slabs):
        density = density + recv_ref[i]
    plane = lax.broadcasted_iota(jnp.int32, (g.slab, g.deep), 0) // g.cols
    lane = lax.broadcasted_iota(jnp.int32, (1, g.deep), 1)
    exponent = jnp.zeros((g.slab, g.deep), jnp.float32)
    rate = jnp.zeros((1, g.deep), jnp.float32)
    for j in range(g.slab_rows):
        exponent = jnp.where(plane == j, bias_ref[j], exponent)
        rate = jnp.where(lane == j, rate_ref[j], rate)
    field = cotangent_of(density, selection_ref[...], counts_ref[...], exponent)
    sent = jnp.concatenate([field, rate], axis=0)
    for i in range(g.slabs):
        out_ref[i * (g.slab + 1) : (i + 1) * (g.slab + 1), :] = sent


def picked(rows, index):
    return jnp.take_along_axis(rows, index, axis=1, mode="promise_in_bounds")


def pull_kernel(
    g, dest_ref, count_ref, cell_ref, frac_ref, offset_ref, field_ref, pos_ref, vel_ref, whole_ref, rate_ref
):
    for i in range(g.slabs):
        start = i * (g.slab + 1)
        whole_ref[i * g.slab : (i + 1) * g.slab, :] = field_ref[start : start + g.slab, :]
        rate_ref[i : i + 1, :] = field_ref[start + g.slab : start + g.slab + 1, :]
    spill = g.window - g.slab
    whole_ref[g.slabs * g.slab :, :] = field_ref[:spill, :]
    plane_iota, sky_iota = row_iotas(g.cols)
    lane = lax.broadcasted_iota(jnp.int32, (1, g.block), 1)
    for k in range(g.blocks):
        slab = dest_ref[k]
        offset = jnp.broadcast_to(offset_ref[k : k + 1, :], (SUB, g.block))
        red = jnp.mod(block_rows(cell_ref, 0, k, g.block) + offset, g.slab_rows)
        sky = block_rows(cell_ref, 1, k, g.block)
        sky_next = jnp.where(sky + 1 == g.sky_wrap, 0, sky + 1)
        deep = block_rows(cell_ref, 2, k, g.block)
        deep_next = jnp.where(deep + 1 == g.deep, 0, deep + 1)
        frac_los = block_rows(frac_ref, 0, k, g.block)
        frac_sky = block_rows(frac_ref, 1, k, g.block)
        frac_deep = block_rows(frac_ref, 2, k, g.block)
        at_sky, at_next = sky_iota == sky, sky_iota == sky_next
        on_sky = jnp.where(at_sky, 1.0 - frac_sky, jnp.where(at_next, frac_sky, 0.0))
        slope_sky = jnp.where(at_next, 1.0, 0.0) - jnp.where(at_sky, 1.0, 0.0)
        sum_val, sum_los, sum_deep = 0.0, 0.0, 0.0
        for i in range(g.window // SUB):
            at = pl.ds(pl.multiple_of(slab * g.slab, SUB) + i * SUB, SUB)
            rows = whole_ref[at, :]
            below = picked(rows, deep)
            step = picked(rows, deep_next) - below
            value = below + frac_deep * step
            plane = plane_iota + i * g.planes_per_tile - red
            at_plane, at_above = plane == 0, plane == 1
            on_los = jnp.where(at_plane, 1.0 - frac_los, jnp.where(at_above, frac_los, 0.0))
            sum_val += on_los * value
            sum_deep += on_los * step
            sum_los += jnp.where(at_above, value, jnp.where(at_plane, -value, 0.0))
        live = lane < count_ref[k]
        lanes = slice(k * g.block, (k + 1) * g.block)
        rate = picked(jnp.broadcast_to(rate_ref[pl.ds(slab, 1), :], (SUB, g.deep)), red)
        grad_los = jnp.where(live, jnp.sum(on_sky * sum_los, axis=0, keepdims=True), 0.0)
        grad_sky = jnp.where(live, jnp.sum(slope_sky * sum_val, axis=0, keepdims=True), 0.0)
        grad_deep = jnp.where(live, jnp.sum(on_sky * sum_deep, axis=0, keepdims=True), 0.0)
        pos_ref[0:1, lanes] = grad_los
        pos_ref[1:2, lanes] = grad_sky
        pos_ref[2:3, lanes] = grad_deep
        vel_ref[k : k + 1, :] = rate[0:1] * grad_los


class Geometry:
    def __init__(self, slabs, sky_parts, cell_shape, block_shape, field_shape):
        self.slabs = slabs
        self.blocks = block_shape[0]
        self.block = cell_shape[1] // self.blocks
        self.slab_rows, self.width, self.deep = field_shape
        self.sky_wrap = self.width if sky_parts == 1 else -1
        need = self.width + (sky_parts > 1)
        self.cols = next(c for c in (1, 2, 4, 8) if c >= need and c * self.slab_rows % SUB == 0)
        self.planes_per_tile = SUB // self.cols
        self.slab = self.slab_rows * self.cols
        self.window = rounded_up(self.slab + self.cols, SUB)


def on_device(
    part_cell,
    part_frac,
    los_offset,
    block_dest,
    block_count,
    selection,
    galaxy_counts,
    bias_exp,
    rsd_factor,
):
    sky_parts = lax.axis_size("sky")
    g = Geometry(
        lax.axis_size("los"), sky_parts, part_cell.shape, block_dest.shape, selection.shape
    )
    f32 = jnp.float32
    smem = pl.BlockSpec(memory_space=pltpu.SMEM)
    vmem = pl.BlockSpec(memory_space=pltpu.VMEM)
    if sky_parts > 1:
        shift = jnp.stack([0, lax.axis_index("sky") * g.width, 0]).astype(jnp.int32)
        part_cell = part_cell - shift[:, None]
    offsets = los_offset.reshape(g.blocks, g.block)
    size = g.slabs * g.slab
    padded = size + g.window - g.slab
    painted = pl.pallas_call(
        functools.partial(paint_kernel, g),
        out_shape=jax.ShapeDtypeStruct((size, g.deep), f32),
        in_specs=[smem, smem, vmem, vmem, vmem],
        out_specs=vmem,
        scratch_shapes=[pltpu.VMEM((padded, g.deep), f32), pltpu.VMEM((padded, g.deep), f32)],
        name="paint",
    )(block_dest, block_count, part_cell, part_frac, offsets)
    recv = exchanged(painted.reshape(g.slabs, g.slab, g.deep))
    tall = g.slabs * (g.slab + 1)
    if sky_parts == 1:
        sent = pl.pallas_call(
            functools.partial(field_kernel, g),
            out_shape=jax.ShapeDtypeStruct((tall, g.deep), f32),
            in_specs=[vmem, vmem, vmem, smem, smem],
            out_specs=vmem,
            name="field",
        )(
            recv,
            selection.reshape(g.slab, g.deep),
            galaxy_counts.reshape(g.slab, g.deep),
            bias_exp,
            rsd_factor,
        )
    else:
        core = jnp.sum(recv, axis=0).reshape(g.slab_rows, g.cols, g.deep)
        density = core[:, : g.width].at[:, 0].add(passed_along(core[:, g.width], "sky", 1))
        field = cotangent_of(density, selection, galaxy_counts, bias_exp[:, None, None])
        rim = passed_along(field[:, 0], "sky", -1)
        rest = jnp.zeros((g.slab_rows, g.cols - g.width - 1, g.deep), f32)
        field = jnp.concatenate([field, rim[:, None], rest], axis=1).reshape(g.slab, g.deep)
        rate = jnp.pad(rsd_factor, (0, g.deep - g.slab_rows))[None]
        sent = jnp.concatenate([field, rate], axis=0)
        sent = jnp.broadcast_to(sent[None], (g.slabs, g.slab + 1, g.deep)).reshape(tall, g.deep)
    whole = exchanged(sent.reshape(g.slabs, 1, (g.slab + 1) * g.deep)).reshape(tall, g.deep)
    grad_pos, grad_vel = pl.pallas_call(
        functools.partial(pull_kernel, g),
        out_shape=(
            jax.ShapeDtypeStruct(part_frac.shape, f32),
            jax.ShapeDtypeStruct((g.blocks, g.block), f32),
        ),
        in_specs=[smem, smem, vmem, vmem, vmem, vmem],
        out_specs=(vmem, vmem),
        scratch_shapes=[pltpu.VMEM((padded, g.deep), f32), pltpu.VMEM((g.slabs, g.deep), f32)],
        name="pull",
    )(block_dest, block_count, part_cell, part_frac, offsets, whole)
    return grad_pos, grad_vel.reshape(-1)


def solution(mesh):
    return jax.shard_map(
        on_device,
        mesh=mesh,
        in_specs=(
            P(None, ("los", "sky")),
            P(None, ("los", "sky")),
            P(("los", "sky")),
            P(("los", "sky")),
            P(("los", "sky")),
            P("los", "sky", None),
            P("los", "sky", None),
            P("los"),
            P("los"),
        ),
        out_specs=(P(None, ("los", "sky")), P(("los", "sky"))),
        check_vma=False,
    )
```

```python
import functools

import jax
import jax.numpy as jnp
from jax import lax
from jax.experimental import pallas as pl
from jax.experimental.pallas import tpu as pltpu
from jax.sharding import PartitionSpec as P

SUB = 8
VMEM_LIMIT = 8 * 1024 * 1024


def passed_along(block, axis, distance):
    devices = range(lax.axis_size(axis))
    route = [((i - distance) % len(devices), i) for i in devices]
    return lax.ppermute(block, axis, route)


def rounded_up(value, step):
    return -(-value // step) * step


def row_iotas(cols):
    sub = lax.broadcasted_iota(jnp.int32, (SUB, 128), 0)
    return sub // cols, sub % cols


def block_rows(ref, row, k, lanes):
    return jnp.broadcast_to(ref[row : row + 1, k * lanes : (k + 1) * lanes], (SUB, lanes))


def slab_at(g, me, near, far):
    return far * g.plane + ((me % g.plane) ^ near)


def write_table(g, refs, table_ref):
    selection_ref, counts_ref, bias_ref, rate_ref = refs
    lane = lax.broadcasted_iota(jnp.int32, (SUB, g.deep), 1)
    rate = jnp.zeros((SUB, g.deep), jnp.float32)
    table_ref[...] = jnp.zeros_like(table_ref)
    for j in range(g.slab_rows):
        rate = jnp.where(lane == j, rate_ref[j], rate)
        start = j * g.cols
        table_ref[start : start + g.width, :] = selection_ref[j]
        table_ref[g.slab + start : g.slab + start + g.width, :] = counts_ref[j].astype(jnp.float32)
        table_ref[2 * g.slab + start : 2 * g.slab + start + g.cols, :] = jnp.full(
            (g.cols, g.deep), bias_ref[j], jnp.float32
        )
    table_ref[3 * g.slab :, :] = rate


def fetch_kernel(g, *refs):
    far_refs, (place_ref, frac_ref, dest_ref, table_ref), near_refs = refs[:9], refs[9:13], refs[13:]
    arrived = near_refs[-1]
    near_refs = (*near_refs[:3], frac_ref, *near_refs[3:-1])
    copies = [
        pltpu.make_async_copy(a, b, arrived.at[i])
        for i, (a, b) in enumerate(zip(far_refs, near_refs, strict=True))
    ]
    for copy in copies:
        copy.start()
    for copy in copies:
        copy.wait()
    blocks_ref, count_ref, cell_ref, frac_ref, offset_ref = near_refs[:5]
    write_table(g, near_refs[5:], table_ref)
    lane = lax.broadcasted_iota(jnp.int32, (1, g.block), 1)
    for k in range(g.blocks):
        lanes = slice(k * g.block, (k + 1) * g.block)
        red = jnp.mod(cell_ref[0:1, lanes] + offset_ref[k : k + 1, :], g.slab_rows)
        deep = jnp.where(lane < count_ref[k], cell_ref[2:3, lanes], -1)
        place_ref[:, lanes] = jnp.concatenate([red, cell_ref[1:2, lanes], deep], axis=0)
        dest_ref[k : k + 1, :] = jnp.full((1, g.deep), blocks_ref[k], jnp.int32)


def dest_of(dest_ref, k):
    return dest_ref[k : k + 1, 0:1][0, 0]


def paint_kernel(g, place_ref, frac_ref, dest_ref, keep_ref, send_ref, low_ref, high_ref):
    low_ref[...] = jnp.zeros_like(low_ref)
    high_ref[...] = jnp.zeros_like(high_ref)
    plane_iota, sky_iota = row_iotas(g.cols)
    deep_iota = lax.broadcasted_iota(jnp.int32, (g.deep, g.block), 0)
    for k in range(g.blocks):
        red = block_rows(place_ref, 0, k, g.block)
        sky = block_rows(place_ref, 1, k, g.block)
        sky_next = jnp.where(sky + 1 == g.sky_wrap, 0, sky + 1)
        frac_los = block_rows(frac_ref, 0, k, g.block)
        frac_sky = block_rows(frac_ref, 1, k, g.block)
        frac_deep = block_rows(frac_ref, 2, k, g.block)
        on_sky = jnp.where(
            sky_iota == sky, 1.0 - frac_sky, jnp.where(sky_iota == sky_next, frac_sky, 0.0)
        )
        rows = []
        for i in range(g.window // SUB):
            plane = plane_iota + i * g.planes_per_tile - red
            on_los = jnp.where(
                plane == 0, 1.0 - frac_los, jnp.where(plane == 1, frac_los, 0.0)
            )
            rows.append(on_los * on_sky)
        weight = jnp.concatenate(rows, axis=0)
        upper = weight * jnp.concatenate([frac_deep] * (g.window // SUB), axis=0)
        weight = jnp.concatenate([weight - upper, upper], axis=0)
        coarse = weight.astype(jnp.bfloat16)
        fine = (weight - coarse.astype(jnp.float32)).astype(jnp.bfloat16)
        deep = jnp.broadcast_to(place_ref[2:3, k * g.block : (k + 1) * g.block], (g.deep, g.block))
        hit = jnp.where(deep_iota == deep, 1.0, 0.0).astype(jnp.bfloat16)
        got = lax.dot_general(
            jnp.concatenate([coarse, fine], axis=0),
            hit,
            (((1,), (1,)), ((), ())),
            preferred_element_type=jnp.float32,
        )
        got = got[: 2 * g.window] + got[2 * g.window :]
        at = pl.ds(pl.multiple_of(dest_of(dest_ref, k) * g.slab, SUB), g.window)
        low_ref[at, :] += got[: g.window]
        high_ref[at, :] += got[g.window :]
    size = g.slabs * g.slab
    spill = g.window - g.slab
    low_ref[:spill, :] += low_ref[size:, :]
    high_ref[:spill, :] += high_ref[size:, :]
    me = lax.axis_index("los")
    for near in range(g.plane):
        for far in range(g.planes):
            at = pl.ds(pl.multiple_of(slab_at(g, me, near, far) * g.slab, SUB), g.slab)
            start = (near // 2) * g.column + far * g.slab
            rows = low_ref[at, :] + pltpu.roll(high_ref[at, :], 1, 1)
            (send_ref if near % 2 else keep_ref)[start : start + g.slab, :] = rows


def cotangent_of(density, selection, counts, exponent):
    shifted = density + 0.5
    intensity = selection * jnp.exp(exponent * jnp.log(shifted))
    return (1.0 - counts.astype(jnp.float32) / intensity) * exponent * intensity / shifted


def field_kernel(g, *refs):
    part_refs, table_refs, out_ref, sum_ref = refs[: g.planes], refs[g.planes : 2 * g.planes], refs[-2], refs[-1]
    total = part_refs[0][...]
    for ref in part_refs[1:]:
        total = total + ref[...]
    sum_ref[...] = total
    far = lax.axis_index("los") // g.plane
    out_ref[g.column :, :] = jnp.zeros((SUB, g.deep), jnp.float32)
    for m, ref in enumerate(table_refs):
        there = lax.rem(far + m, g.planes)
        at = pl.ds(pl.multiple_of(there * g.slab, SUB), g.slab)
        out_ref[at, :] = cotangent_of(
            sum_ref[at, :], ref[: g.slab, :], ref[g.slab : 2 * g.slab, :], ref[2 * g.slab : 3 * g.slab, :]
        )
        out_ref[pl.ds(g.column + there, 1), :] = ref[3 * g.slab : 3 * g.slab + 1, :]


def picked(rows, index):
    return jnp.take_along_axis(rows, index, axis=1, mode="promise_in_bounds")


def pull_kernel(g, place_ref, frac_ref, dest_ref, *refs):
    field_refs, (pos_ref, vel_ref, whole_ref, rate_ref) = refs[:-4], refs[-4:]
    me = lax.axis_index("los")
    tall = g.column + SUB
    for near in range(g.plane):
        ref, base = field_refs[near // 2], (near % 2) * tall
        for far in range(g.planes):
            slab = slab_at(g, me, near, far)
            at = pl.ds(pl.multiple_of(slab * g.slab, SUB), g.slab)
            start = base + far * g.slab
            whole_ref[at, :] = ref[start : start + g.slab, :]
            start = base + g.column + far
            rate_ref[pl.ds(slab, 1), :] = ref[start : start + 1, :]
    spill = g.window - g.slab
    whole_ref[g.slabs * g.slab :, :] = whole_ref[:spill, :]
    plane_iota, sky_iota = row_iotas(g.cols)
    for k in range(g.blocks):
        slab = dest_of(dest_ref, k)
        red = block_rows(place_ref, 0, k, g.block)
        sky = block_rows(place_ref, 1, k, g.block)
        sky_next = jnp.where(sky + 1 == g.sky_wrap, 0, sky + 1)
        deep = block_rows(place_ref, 2, k, g.block)
        live = deep[0:1] >= 0
        deep = jnp.maximum(deep, 0)
        deep_next = jnp.where(deep + 1 == g.deep, 0, deep + 1)
        frac_los = block_rows(frac_ref, 0, k, g.block)
        frac_sky = block_rows(frac_ref, 1, k, g.block)
        frac_deep = block_rows(frac_ref, 2, k, g.block)
        at_sky, at_next = sky_iota == sky, sky_iota == sky_next
        on_sky = jnp.where(at_sky, 1.0 - frac_sky, jnp.where(at_next, frac_sky, 0.0))
        slope_sky = jnp.where(at_next, 1.0, 0.0) - jnp.where(at_sky, 1.0, 0.0)
        sum_val, sum_los, sum_deep = 0.0, 0.0, 0.0
        for i in range(g.window // SUB):
            at = pl.ds(pl.multiple_of(slab * g.slab, SUB) + i * SUB, SUB)
            rows = whole_ref[at, :]
            below = picked(rows, deep)
            step = picked(rows, deep_next) - below
            value = below + frac_deep * step
            plane = plane_iota + i * g.planes_per_tile - red
            at_plane, at_above = plane == 0, plane == 1
            on_los = jnp.where(at_plane, 1.0 - frac_los, jnp.where(at_above, frac_los, 0.0))
            sum_val += on_los * value
            sum_deep += on_los * step
            sum_los += jnp.where(at_above, value, jnp.where(at_plane, -value, 0.0))
        lanes = slice(k * g.block, (k + 1) * g.block)
        rate = picked(jnp.broadcast_to(rate_ref[pl.ds(slab, 1), :], (SUB, g.deep)), red)
        grad_los = jnp.where(live, jnp.sum(on_sky * sum_los, axis=0, keepdims=True), 0.0)
        grad_sky = jnp.where(live, jnp.sum(slope_sky * sum_val, axis=0, keepdims=True), 0.0)
        grad_deep = jnp.where(live, jnp.sum(on_sky * sum_deep, axis=0, keepdims=True), 0.0)
        pos_ref[0:1, lanes] = grad_los
        pos_ref[1:2, lanes] = grad_sky
        pos_ref[2:3, lanes] = grad_deep
        vel_ref[k : k + 1, :] = rate[0:1] * grad_los


class Geometry:
    def __init__(self, slabs, sky_parts, cell_shape, block_shape, field_shape):
        self.slabs = slabs
        self.blocks = block_shape[0]
        self.block = cell_shape[1] // self.blocks
        self.slab_rows, self.width, self.deep = field_shape
        self.sky_wrap = self.width if sky_parts == 1 else -1
        need = self.width + (sky_parts > 1)
        self.cols = next(c for c in (1, 2, 4, 8) if c >= need and c * self.slab_rows % SUB == 0)
        self.planes_per_tile = SUB // self.cols
        self.slab = self.slab_rows * self.cols
        self.plane = 8
        self.planes = slabs // self.plane
        self.column = self.planes * self.slab
        self.window = rounded_up(self.slab + self.cols, SUB)


def on_device(
    part_cell,
    part_frac,
    los_offset,
    block_dest,
    block_count,
    selection,
    galaxy_counts,
    bias_exp,
    rsd_factor,
):
    sky_parts = lax.axis_size("sky")
    g = Geometry(
        lax.axis_size("los"), sky_parts, part_cell.shape, block_dest.shape, selection.shape
    )
    f32 = jnp.float32
    vmem = pl.BlockSpec(memory_space=pltpu.VMEM)
    if sky_parts > 1:
        shift = jnp.stack([0, lax.axis_index("sky") * g.width, 0]).astype(jnp.int32)
        part_cell = part_cell - shift[:, None]
    offsets = los_offset.reshape(g.blocks, g.block)
    size = g.slabs * g.slab
    padded = size + g.window - g.slab
    small = pltpu.CompilerParams(vmem_limit_bytes=VMEM_LIMIT)

    def tiled(rows):
        return jax.ShapeDtypeStruct((rows, g.deep), f32)

    def to_near(block, near):
        return lax.ppermute(block, "los", [(i ^ near, i) for i in range(g.slabs)])

    def from_far(block, m):
        return passed_along(block, "los", -m * g.plane)

    given = (
        block_dest,
        block_count,
        part_cell,
        part_frac,
        offsets,
        selection,
        galaxy_counts,
        bias_exp,
        rsd_factor,
    )
    place, frac, dest, table = pl.pallas_call(
        functools.partial(fetch_kernel, g),
        out_shape=(
            pltpu.VMEM(part_cell.shape, jnp.int32),
            pltpu.VMEM(part_frac.shape, f32),
            pltpu.VMEM((g.blocks, g.deep), jnp.int32),
            pltpu.VMEM((3 * g.slab + SUB, g.deep), f32),
        ),
        in_specs=[pl.BlockSpec(memory_space=pltpu.HBM)] * len(given),
        out_specs=(vmem,) * 4,
        scratch_shapes=[
            pltpu.SMEM(block_dest.shape, jnp.int32),
            pltpu.SMEM(block_count.shape, jnp.int32),
            pltpu.VMEM(part_cell.shape, jnp.int32),
            pltpu.VMEM(offsets.shape, jnp.int32),
            pltpu.VMEM(selection.shape, f32),
            pltpu.VMEM(galaxy_counts.shape, jnp.int32),
            pltpu.SMEM(bias_exp.shape, f32),
            pltpu.SMEM(rsd_factor.shape, f32),
            pltpu.SemaphoreType.DMA((len(given),)),
        ],
        compiler_params=small,
        name="fetch",
    )(*(pltpu.with_memory_space_constraint(x, pltpu.HBM) for x in given))
    keep, send = pl.pallas_call(
        functools.partial(paint_kernel, g),
        out_shape=(tiled(size // 2), tiled(size // 2)),
        in_specs=[vmem] * 3,
        out_specs=(vmem, vmem),
        scratch_shapes=[pltpu.VMEM((padded, g.deep), f32), pltpu.VMEM((padded, g.deep), f32)],
        compiler_params=small,
        cost_estimate=pl.CostEstimate(flops=10**9, bytes_accessed=10**7, transcendentals=0),
        name="paint",
    )(place, frac, dest)
    tables = [table] + [from_far(table, m) for m in range(1, g.planes)]
    quarters = g.plane // 2
    pair = (keep + to_near(send, 1)).reshape(quarters, g.column, g.deep)
    column = pair[0] + sum(to_near(pair[j], 2 * j) for j in range(1, quarters))
    parts = [column] + [from_far(column, m) for m in range(1, g.planes)]
    tall = g.column + SUB
    if sky_parts == 1:
        field = pl.pallas_call(
            functools.partial(field_kernel, g),
            out_shape=tiled(tall),
            in_specs=[vmem] * (2 * g.planes),
            out_specs=vmem,
            scratch_shapes=[pltpu.VMEM((g.column, g.deep), f32)],
            compiler_params=small,
            name="field",
        )(*parts, *tables)
    else:
        start = jnp.mod(-(lax.axis_index("los") // g.plane), g.planes)
        planes = lax.dynamic_slice_in_dim(jnp.stack(tables + tables), start, g.planes)
        cells = planes[:, : 3 * g.slab].reshape(g.planes, 3, g.slab_rows, g.cols, g.deep)
        core = sum(parts).reshape(g.planes, g.slab_rows, g.cols, g.deep)
        edge = passed_along(core[:, :, g.width], "sky", 1)
        density = core[:, :, : g.width].at[:, :, 0].add(edge)
        near = cells[:, :, :, : g.width]
        inner = cotangent_of(density, near[:, 0], near[:, 1], near[:, 2])
        rim = passed_along(inner[:, :, 0], "sky", -1)
        rest = jnp.zeros((g.planes, g.slab_rows, g.cols - g.width - 1, g.deep), f32)
        inner = jnp.concatenate([inner, rim[:, :, None], rest], axis=2).reshape(g.column, g.deep)
        rates = jnp.pad(planes[:, 3 * g.slab], ((0, SUB - g.planes), (0, 0)))
        field = jnp.concatenate([inner, rates])
    both = jnp.concatenate([field, to_near(field, 1)])
    fields = [both] + [to_near(both, 2 * j) for j in range(1, quarters)]
    grad_pos, grad_vel = pl.pallas_call(
        functools.partial(pull_kernel, g),
        out_shape=(
            jax.ShapeDtypeStruct(part_frac.shape, f32),
            jax.ShapeDtypeStruct((g.blocks, g.block), f32),
        ),
        in_specs=[vmem] * (3 + quarters),
        out_specs=(vmem, vmem),
        scratch_shapes=[pltpu.VMEM((padded, g.deep), f32), pltpu.VMEM((g.slabs, g.deep), f32)],
        compiler_params=small,
        name="pull",
    )(place, frac, dest, *fields)
    return grad_pos, grad_vel.reshape(-1)


def solution(mesh):
    return jax.shard_map(
        on_device,
        mesh=mesh,
        in_specs=(
            P(None, ("los", "sky")),
            P(None, ("los", "sky")),
            P(("los", "sky")),
            P(("los", "sky")),
            P(("los", "sky")),
            P("los", "sky", None),
            P("los", "sky", None),
            P("los"),
            P("los"),
        ),
        out_specs=(P(None, ("los", "sky")), P(("los", "sky"))),
        check_vma=False,
    )
```

```python
import functools

import jax
import jax.numpy as jnp
from jax import lax
from jax.experimental import pallas as pl
from jax.experimental.pallas import tpu as pltpu
from jax.sharding import PartitionSpec as P

SUB = 8
VMEM_LIMIT = 8 * 1024 * 1024


def passed_along(block, axis, distance):
    devices = range(lax.axis_size(axis))
    route = [((i - distance) % len(devices), i) for i in devices]
    return lax.ppermute(block, axis, route)


def rounded_up(value, step):
    return -(-value // step) * step


def row_iotas(cols):
    sub = lax.broadcasted_iota(jnp.int32, (SUB, 128), 0)
    return sub // cols, sub % cols


def block_rows(ref, row, k, lanes):
    return jnp.broadcast_to(ref[row : row + 1, k * lanes : (k + 1) * lanes], (SUB, lanes))


def slab_at(g, me, near, far):
    return far * g.plane + ((me % g.plane) ^ near)


def write_table(g, refs, table_ref):
    selection_ref, counts_ref, bias_ref, rate_ref = refs
    sub = lax.broadcasted_iota(jnp.int32, (SUB, g.deep), 0)
    lane = lax.broadcasted_iota(jnp.int32, (SUB, g.deep), 1)
    rest = jnp.zeros((SUB, g.deep), jnp.float32)
    table_ref[...] = jnp.zeros_like(table_ref)
    for j in range(g.slab_rows):
        rest = jnp.where(lane == j, jnp.where(sub == 0, bias_ref[j], rate_ref[j]), rest)
        start = j * g.cols
        table_ref[start : start + g.width, :] = selection_ref[j]
        table_ref[g.slab + start : g.slab + start + g.width, :] = counts_ref[j].astype(jnp.float32)
    table_ref[2 * g.slab :, :] = rest


def fetch_kernel(g, *refs):
    far_refs, (place_ref, frac_ref, dest_ref, table_ref), near_refs = refs[:9], refs[9:13], refs[13:]
    arrived = near_refs[-1]
    near_refs = (*near_refs[:3], frac_ref, *near_refs[3:-1])
    copies = [
        pltpu.make_async_copy(a, b, arrived.at[i])
        for i, (a, b) in enumerate(zip(far_refs, near_refs, strict=True))
    ]
    for copy in copies:
        copy.start()
    for copy in copies:
        copy.wait()
    blocks_ref, count_ref, cell_ref, frac_ref, offset_ref = near_refs[:5]
    write_table(g, near_refs[5:], table_ref)
    lane = lax.broadcasted_iota(jnp.int32, (1, g.block), 1)
    for k in range(g.blocks):
        lanes = slice(k * g.block, (k + 1) * g.block)
        red = jnp.mod(cell_ref[0:1, lanes] + offset_ref[k : k + 1, :], g.slab_rows)
        deep = jnp.where(lane < count_ref[k], cell_ref[2:3, lanes], -1)
        place_ref[:, lanes] = jnp.concatenate([red, cell_ref[1:2, lanes], deep], axis=0)
        dest_ref[k : k + 1, :] = jnp.full((1, g.deep), blocks_ref[k], jnp.int32)


def dest_of(dest_ref, k):
    return dest_ref[k : k + 1, 0:1][0, 0]


def paint_kernel(g, place_ref, frac_ref, dest_ref, keep_ref, send_ref, low_ref, high_ref):
    low_ref[...] = jnp.zeros_like(low_ref)
    high_ref[...] = jnp.zeros_like(high_ref)
    plane_iota, sky_iota = row_iotas(g.cols)
    deep_iota = lax.broadcasted_iota(jnp.int32, (g.deep, g.block), 0)
    for k in range(g.blocks):
        red = block_rows(place_ref, 0, k, g.block)
        sky = block_rows(place_ref, 1, k, g.block)
        sky_next = jnp.where(sky + 1 == g.sky_wrap, 0, sky + 1)
        frac_los = block_rows(frac_ref, 0, k, g.block)
        frac_sky = block_rows(frac_ref, 1, k, g.block)
        frac_deep = block_rows(frac_ref, 2, k, g.block)
        on_sky = jnp.where(
            sky_iota == sky, 1.0 - frac_sky, jnp.where(sky_iota == sky_next, frac_sky, 0.0)
        )
        rows = []
        for i in range(g.window // SUB):
            plane = plane_iota + i * g.planes_per_tile - red
            on_los = jnp.where(
                plane == 0, 1.0 - frac_los, jnp.where(plane == 1, frac_los, 0.0)
            )
            rows.append(on_los * on_sky)
        weight = jnp.concatenate(rows, axis=0)
        upper = weight * jnp.concatenate([frac_deep] * (g.window // SUB), axis=0)
        weight = jnp.concatenate([weight - upper, upper], axis=0)
        coarse = weight.astype(jnp.bfloat16)
        fine = (weight - coarse.astype(jnp.float32)).astype(jnp.bfloat16)
        deep = jnp.broadcast_to(place_ref[2:3, k * g.block : (k + 1) * g.block], (g.deep, g.block))
        hit = jnp.where(deep_iota == deep, 1.0, 0.0).astype(jnp.bfloat16)
        got = lax.dot_general(
            jnp.concatenate([coarse, fine], axis=0),
            hit,
            (((1,), (1,)), ((), ())),
            preferred_element_type=jnp.float32,
        )
        got = got[: 2 * g.window] + got[2 * g.window :]
        at = pl.ds(pl.multiple_of(dest_of(dest_ref, k) * g.slab, SUB), g.window)
        low_ref[at, :] += got[: g.window]
        high_ref[at, :] += got[g.window :]
    size = g.slabs * g.slab
    spill = g.window - g.slab
    low_ref[:spill, :] += low_ref[size:, :]
    high_ref[:spill, :] += high_ref[size:, :]
    me = lax.axis_index("los")
    for near in range(g.plane):
        for far in range(g.planes):
            at = pl.ds(pl.multiple_of(slab_at(g, me, near, far) * g.slab, SUB), g.slab)
            start = (near // 2) * g.column + far * g.slab
            rows = low_ref[at, :] + pltpu.roll(high_ref[at, :], 1, 1)
            (send_ref if near % 2 else keep_ref)[start : start + g.slab, :] = rows


def cotangent_of(density, selection, counts, exponent):
    shifted = density + 0.5
    intensity = selection * jnp.exp(exponent * jnp.log(shifted))
    return (1.0 - counts.astype(jnp.float32) / intensity) * exponent * intensity / shifted


def column_kernel(g, own_ref, *refs):
    total = own_ref[...]
    for ref in refs[:-2]:
        total = total + ref[...]
    refs[-1][: g.column, :] = total
    refs[-1][g.column :, :] = refs[-2][...]


def field_kernel(g, *refs):
    part_refs, out_ref, sum_ref = refs[: g.planes], refs[-2], refs[-1]
    total = part_refs[0][: g.column, :]
    for ref in part_refs[1:]:
        total = total + ref[: g.column, :]
    sum_ref[...] = total
    far = lax.axis_index("los") // g.plane
    plane = lax.broadcasted_iota(jnp.int32, (g.slab, g.deep), 0) // g.cols
    out_ref[g.column :, :] = jnp.zeros((SUB, g.deep), jnp.float32)
    for m, ref in enumerate(part_refs):
        there = g.far_peer(far, m)
        at = pl.ds(pl.multiple_of(there * g.slab, SUB), g.slab)
        start = g.column + 2 * g.slab
        exponent = picked(jnp.broadcast_to(ref[start : start + 1, :], (g.slab, g.deep)), plane)
        selection = ref[g.column : g.column + g.slab, :]
        counts = ref[g.column + g.slab : start, :]
        out_ref[at, :] = cotangent_of(sum_ref[at, :], selection, counts, exponent)
        out_ref[pl.ds(g.column + there, 1), :] = ref[start + 1 : start + 2, :]


def joined_kernel(*refs):
    rows = refs[0].shape[0]
    for i, ref in enumerate(refs[:-1]):
        refs[-1][i * rows : (i + 1) * rows, :] = ref[...]


def picked(rows, index):
    return jnp.take_along_axis(rows, index, axis=1, mode="promise_in_bounds")


def pull_kernel(g, place_ref, frac_ref, dest_ref, *refs):
    field_refs, (pos_ref, vel_ref, whole_ref, rate_ref) = refs[:-4], refs[-4:]
    me = lax.axis_index("los")
    tall = g.column + SUB
    for near in range(g.plane):
        ref, base = field_refs[near % 2], (near // 2) * tall
        for far in range(g.planes):
            slab = slab_at(g, me, near, far)
            at = pl.ds(pl.multiple_of(slab * g.slab, SUB), g.slab)
            start = base + far * g.slab
            whole_ref[at, :] = ref[start : start + g.slab, :]
            start = base + g.column + far
            rate_ref[pl.ds(slab, 1), :] = ref[start : start + 1, :]
    spill = g.window - g.slab
    whole_ref[g.slabs * g.slab :, :] = whole_ref[:spill, :]
    plane_iota, sky_iota = row_iotas(g.cols)
    for k in range(g.blocks):
        slab = dest_of(dest_ref, k)
        red = block_rows(place_ref, 0, k, g.block)
        sky = block_rows(place_ref, 1, k, g.block)
        sky_next = jnp.where(sky + 1 == g.sky_wrap, 0, sky + 1)
        deep = block_rows(place_ref, 2, k, g.block)
        live = deep[0:1] >= 0
        deep = jnp.maximum(deep, 0)
        deep_next = jnp.where(deep + 1 == g.deep, 0, deep + 1)
        frac_los = block_rows(frac_ref, 0, k, g.block)
        frac_sky = block_rows(frac_ref, 1, k, g.block)
        frac_deep = block_rows(frac_ref, 2, k, g.block)
        at_sky, at_next = sky_iota == sky, sky_iota == sky_next
        on_sky = jnp.where(at_sky, 1.0 - frac_sky, jnp.where(at_next, frac_sky, 0.0))
        slope_sky = jnp.where(at_next, 1.0, 0.0) - jnp.where(at_sky, 1.0, 0.0)
        sum_val, sum_los, sum_deep = 0.0, 0.0, 0.0
        for i in range(g.window // SUB):
            at = pl.ds(pl.multiple_of(slab * g.slab, SUB) + i * SUB, SUB)
            rows = whole_ref[at, :]
            below = picked(rows, deep)
            step = picked(rows, deep_next) - below
            value = below + frac_deep * step
            plane = plane_iota + i * g.planes_per_tile - red
            at_plane, at_above = plane == 0, plane == 1
            on_los = jnp.where(at_plane, 1.0 - frac_los, jnp.where(at_above, frac_los, 0.0))
            sum_val += on_los * value
            sum_deep += on_los * step
            sum_los += jnp.where(at_above, value, jnp.where(at_plane, -value, 0.0))
        lanes = slice(k * g.block, (k + 1) * g.block)
        rate = picked(jnp.broadcast_to(rate_ref[pl.ds(slab, 1), :], (SUB, g.deep)), red)
        grad_los = jnp.where(live, jnp.sum(on_sky * sum_los, axis=0, keepdims=True), 0.0)
        grad_sky = jnp.where(live, jnp.sum(slope_sky * sum_val, axis=0, keepdims=True), 0.0)
        grad_deep = jnp.where(live, jnp.sum(on_sky * sum_deep, axis=0, keepdims=True), 0.0)
        pos_ref[0:1, lanes] = grad_los
        pos_ref[1:2, lanes] = grad_sky
        pos_ref[2:3, lanes] = grad_deep
        vel_ref[k : k + 1, :] = rate[0:1] * grad_los


class Geometry:
    def __init__(self, slabs, sky_parts, cell_shape, block_shape, field_shape):
        self.slabs = slabs
        self.blocks = block_shape[0]
        self.block = cell_shape[1] // self.blocks
        self.slab_rows, self.width, self.deep = field_shape
        self.sky_wrap = self.width if sky_parts == 1 else -1
        need = self.width + (sky_parts > 1)
        self.cols = next(c for c in (1, 2, 4, 8) if c >= need and c * self.slab_rows % SUB == 0)
        self.planes_per_tile = SUB // self.cols
        self.slab = self.slab_rows * self.cols
        self.plane = 8
        self.planes = slabs // self.plane
        self.column = self.planes * self.slab
        self.window = rounded_up(self.slab + self.cols, SUB)

    def far_peer(self, far, m):
        even = self.planes & (self.planes - 1) == 0
        return far ^ m if even else (far + m) % self.planes


def on_device(
    part_cell,
    part_frac,
    los_offset,
    block_dest,
    block_count,
    selection,
    galaxy_counts,
    bias_exp,
    rsd_factor,
):
    sky_parts = lax.axis_size("sky")
    g = Geometry(
        lax.axis_size("los"), sky_parts, part_cell.shape, block_dest.shape, selection.shape
    )
    f32 = jnp.float32
    vmem = pl.BlockSpec(memory_space=pltpu.VMEM)
    if sky_parts > 1:
        shift = jnp.stack([0, lax.axis_index("sky") * g.width, 0]).astype(jnp.int32)
        part_cell = part_cell - shift[:, None]
    offsets = los_offset.reshape(g.blocks, g.block)
    size = g.slabs * g.slab
    padded = size + g.window - g.slab
    small = pltpu.CompilerParams(vmem_limit_bytes=VMEM_LIMIT)

    def tiled(rows):
        return jax.ShapeDtypeStruct((rows, g.deep), f32)

    def to_near(block, near):
        return lax.ppermute(block, "los", [(i ^ near, i) for i in range(g.slabs)])

    def from_far(block, m):
        rest = [(i // g.plane, i % g.plane) for i in range(g.slabs)]
        route = [(g.far_peer(far, m) * g.plane + near, far * g.plane + near) for far, near in rest]
        return lax.ppermute(block, "los", route)

    given = (
        block_dest,
        block_count,
        part_cell,
        part_frac,
        offsets,
        selection,
        galaxy_counts,
        bias_exp,
        rsd_factor,
    )
    place, frac, dest, table = pl.pallas_call(
        functools.partial(fetch_kernel, g),
        out_shape=(
            pltpu.VMEM(part_cell.shape, jnp.int32),
            pltpu.VMEM(part_frac.shape, f32),
            pltpu.VMEM((g.blocks, g.deep), jnp.int32),
            pltpu.VMEM((2 * g.slab + SUB, g.deep), f32),
        ),
        in_specs=[pl.BlockSpec(memory_space=pltpu.HBM)] * len(given),
        out_specs=(vmem,) * 4,
        scratch_shapes=[
            pltpu.SMEM(block_dest.shape, jnp.int32),
            pltpu.SMEM(block_count.shape, jnp.int32),
            pltpu.VMEM(part_cell.shape, jnp.int32),
            pltpu.VMEM(offsets.shape, jnp.int32),
            pltpu.VMEM(selection.shape, f32),
            pltpu.VMEM(galaxy_counts.shape, jnp.int32),
            pltpu.SMEM(bias_exp.shape, f32),
            pltpu.SMEM(rsd_factor.shape, f32),
            pltpu.SemaphoreType.DMA((len(given),)),
        ],
        compiler_params=small,
        name="fetch",
    )(*(pltpu.with_memory_space_constraint(x, pltpu.HBM) for x in given))
    keep, send = pl.pallas_call(
        functools.partial(paint_kernel, g),
        out_shape=(tiled(size // 2), tiled(size // 2)),
        in_specs=[vmem] * 3,
        out_specs=(vmem, vmem),
        scratch_shapes=[pltpu.VMEM((padded, g.deep), f32), pltpu.VMEM((padded, g.deep), f32)],
        compiler_params=small,
        cost_estimate=pl.CostEstimate(flops=10**9, bytes_accessed=10**7, transcendentals=0),
        name="paint",
    )(place, frac, dest)
    quarters = g.plane // 2
    pair = (keep + to_near(send, 1)).reshape(quarters, g.column, g.deep)
    column = pl.pallas_call(
        functools.partial(column_kernel, g),
        out_shape=tiled(g.column + 2 * g.slab + SUB),
        in_specs=[vmem] * (quarters + 1),
        out_specs=vmem,
        compiler_params=small,
        name="column",
    )(pair[0], *(to_near(pair[j], 2 * j) for j in range(1, quarters)), table)
    parts = [column] + [from_far(column, m) for m in range(1, g.planes)]
    tall = g.column + SUB
    if sky_parts == 1:
        field = pl.pallas_call(
            functools.partial(field_kernel, g),
            out_shape=tiled(tall),
            in_specs=[vmem] * g.planes,
            out_specs=vmem,
            scratch_shapes=[pltpu.VMEM((g.column, g.deep), f32)],
            compiler_params=small,
            name="field",
        )(*parts)
    else:
        here = lax.axis_index("los") // g.plane
        stacked = jnp.stack(parts)
        planes = jnp.zeros_like(stacked[:, g.column :])
        for m in range(g.planes):
            planes = lax.dynamic_update_index_in_dim(
                planes, stacked[m, g.column :], g.far_peer(here, m), 0
            )
        cells = planes[:, : 2 * g.slab].reshape(g.planes, 2, g.slab_rows, g.cols, g.deep)
        power = planes[:, 2 * g.slab, : g.slab_rows, None, None]
        core = jnp.sum(stacked[:, : g.column], axis=0)
        core = core.reshape(g.planes, g.slab_rows, g.cols, g.deep)
        edge = passed_along(core[:, :, g.width], "sky", 1)
        density = core[:, :, : g.width].at[:, :, 0].add(edge)
        near = cells[:, :, :, : g.width]
        inner = cotangent_of(density, near[:, 0], near[:, 1], power)
        rim = passed_along(inner[:, :, 0], "sky", -1)
        rest = jnp.zeros((g.planes, g.slab_rows, g.cols - g.width - 1, g.deep), f32)
        inner = jnp.concatenate([inner, rim[:, :, None], rest], axis=2).reshape(g.column, g.deep)
        rates = jnp.pad(planes[:, 2 * g.slab + 1], ((0, SUB - g.planes), (0, 0)))
        field = jnp.concatenate([inner, rates])
    even = pl.pallas_call(
        joined_kernel,
        out_shape=tiled(quarters * tall),
        in_specs=[vmem] * quarters,
        out_specs=vmem,
        compiler_params=small,
        name="joined",
    )(field, *(to_near(field, 2 * j) for j in range(1, quarters)))
    fields = [even, to_near(even, 1)]
    grad_pos, grad_vel = pl.pallas_call(
        functools.partial(pull_kernel, g),
        out_shape=(
            jax.ShapeDtypeStruct(part_frac.shape, f32),
            jax.ShapeDtypeStruct((g.blocks, g.block), f32),
        ),
        in_specs=[vmem] * 5,
        out_specs=(vmem, vmem),
        scratch_shapes=[pltpu.VMEM((padded, g.deep), f32), pltpu.VMEM((g.slabs, g.deep), f32)],
        compiler_params=small,
        name="pull",
    )(place, frac, dest, *fields)
    return grad_pos, grad_vel.reshape(-1)


def solution(mesh):
    return jax.shard_map(
        on_device,
        mesh=mesh,
        in_specs=(
            P(None, ("los", "sky")),
            P(None, ("los", "sky")),
            P(("los", "sky")),
            P(("los", "sky")),
            P(("los", "sky")),
            P("los", "sky", None),
            P("los", "sky", None),
            P("los"),
            P("los"),
        ),
        out_specs=(P(None, ("los", "sky")), P(("los", "sky"))),
        check_vma=False,
    )
```

```python
import functools

import jax
import jax.numpy as jnp
from jax import lax
from jax.experimental import pallas as pl
from jax.experimental.pallas import tpu as pltpu
from jax.sharding import PartitionSpec as P

SUB = 8
VMEM_LIMIT = 8 * 1024 * 1024


def passed_along(block, axis, distance):
    devices = range(lax.axis_size(axis))
    route = [((i - distance) % len(devices), i) for i in devices]
    return lax.ppermute(block, axis, route)


def rounded_up(value, step):
    return -(-value // step) * step


def row_iotas(cols):
    sub = lax.broadcasted_iota(jnp.int32, (SUB, 128), 0)
    return sub // cols, sub % cols


def block_rows(ref, row, k, lanes):
    return jnp.broadcast_to(ref[row : row + 1, k * lanes : (k + 1) * lanes], (SUB, lanes))


def slab_at(g, me, near, far):
    return far * g.plane + ((me % g.plane) ^ near)


def write_table(g, refs, table_ref):
    selection_ref, counts_ref, bias_ref, rate_ref = refs
    sub = lax.broadcasted_iota(jnp.int32, (SUB, g.deep), 0)
    lane = lax.broadcasted_iota(jnp.int32, (SUB, g.deep), 1)
    rest = jnp.zeros((SUB, g.deep), jnp.float32)
    table_ref[...] = jnp.zeros_like(table_ref)
    for j in range(g.slab_rows):
        rest = jnp.where(lane == j, jnp.where(sub == 0, bias_ref[j], rate_ref[j]), rest)
        start = j * g.cols
        table_ref[start : start + g.width, :] = selection_ref[j]
        table_ref[g.slab + start : g.slab + start + g.width, :] = counts_ref[j].astype(jnp.float32)
    table_ref[2 * g.slab :, :] = rest


def started(sources, targets, arrived):
    copies = [
        pltpu.make_async_copy(a, b, arrived.at[i])
        for i, (a, b) in enumerate(zip(sources, targets, strict=True))
    ]
    for copy in copies:
        copy.start()
    return copies


def dest_of(dest_ref, k):
    return dest_ref[k : k + 1, 0:1][0, 0]


def red_of(g, cell, offset):
    even = g.slab_rows & (g.slab_rows - 1) == 0
    return (cell + offset) & (g.slab_rows - 1) if even else jnp.mod(cell + offset, g.slab_rows)


def paint_kernel(g, *refs):
    far_refs, (cell_ref, frac_ref, offset_ref, keep_ref, send_ref), refs = refs[:5], refs[5:10], refs[10:]
    dest_ref, count_ref, low_ref, high_ref, arrived = refs
    copies = started(far_refs, (dest_ref, count_ref, cell_ref, frac_ref, offset_ref), arrived)
    low_ref[...] = jnp.zeros_like(low_ref)
    high_ref[...] = jnp.zeros_like(high_ref)
    for copy in copies:
        copy.wait()
    lane = lax.broadcasted_iota(jnp.int32, (SUB, g.block), 1)
    plane_iota, sky_iota = row_iotas(g.cols)
    deep_iota = lax.broadcasted_iota(jnp.int32, (g.deep, g.block), 0)
    deep_iota = deep_iota.astype(jnp.float32).astype(g.cell_type)
    for k in range(g.blocks):
        offset = jnp.broadcast_to(offset_ref[k : k + 1, :], (SUB, g.block))
        red = red_of(g, block_rows(cell_ref, 0, k, g.block), offset)
        sky = block_rows(cell_ref, 1, k, g.block)
        sky_next = jnp.where(sky + 1 == g.sky_wrap, 0, sky + 1)
        frac_los = block_rows(frac_ref, 0, k, g.block)
        frac_sky = block_rows(frac_ref, 1, k, g.block)
        frac_deep = block_rows(frac_ref, 2, k, g.block)
        on_sky = jnp.where(
            sky_iota == sky, 1.0 - frac_sky, jnp.where(sky_iota == sky_next, frac_sky, 0.0)
        )
        on_sky = jnp.where(lane < count_ref[k], on_sky, 0.0)
        rows = []
        for i in range(g.window // SUB):
            plane = plane_iota + i * g.planes_per_tile - red
            on_los = jnp.where(
                plane == 0, 1.0 - frac_los, jnp.where(plane == 1, frac_los, 0.0)
            )
            rows.append(on_los * on_sky)
        weight = jnp.concatenate(rows, axis=0)
        upper = weight * jnp.concatenate([frac_deep] * (g.window // SUB), axis=0)
        weight = jnp.concatenate([weight - upper, upper], axis=0)
        coarse = weight.astype(jnp.bfloat16)
        fine = (weight - coarse.astype(jnp.float32)).astype(jnp.bfloat16)
        deep = cell_ref[2:3, k * g.block : (k + 1) * g.block].astype(jnp.float32)
        hit = deep_iota == jnp.broadcast_to(deep.astype(g.cell_type), (g.deep, g.block))
        one, zero = jnp.ones_like(deep_iota), jnp.zeros_like(deep_iota)
        hit = jnp.where(hit, one, zero).astype(jnp.bfloat16)
        got = lax.dot_general(
            jnp.concatenate([coarse, fine], axis=0),
            hit,
            (((1,), (1,)), ((), ())),
            preferred_element_type=jnp.float32,
        )
        got = got[: 2 * g.window] + got[2 * g.window :]
        at = pl.ds(pl.multiple_of(dest_ref[k] * g.slab, SUB), g.window)
        low_ref[at, :] += got[: g.window]
        high_ref[at, :] += got[g.window :]
    size = g.slabs * g.slab
    spill = g.window - g.slab
    low_ref[:spill, :] += low_ref[size:, :]
    high_ref[:spill, :] += high_ref[size:, :]
    me = lax.axis_index("los")
    for near in range(g.plane):
        for far in range(g.planes):
            at = pl.ds(pl.multiple_of(slab_at(g, me, near, far) * g.slab, SUB), g.slab)
            start = (near // 2) * g.column + far * g.slab
            rows = low_ref[at, :] + pltpu.roll(high_ref[at, :], 1, 1)
            (send_ref if near % 2 else keep_ref)[start : start + g.slab, :] = rows


def cotangent_of(density, selection, counts, exponent):
    shifted = density + 0.5
    intensity = selection * jnp.exp(exponent * jnp.log(shifted))
    return (1.0 - counts.astype(jnp.float32) / intensity) * exponent * intensity / shifted


def column_kernel(g, own_ref, *refs):
    total = own_ref[...]
    for ref in refs[:-2]:
        total = total + ref[...]
    refs[-1][: g.column, :] = total
    refs[-1][g.column :, :] = refs[-2][...]


def field_kernel(g, *refs):
    part_refs, out_ref, sum_ref = refs[: g.planes], refs[-2], refs[-1]
    total = part_refs[0][: g.column, :]
    for ref in part_refs[1:]:
        total = total + ref[: g.column, :]
    sum_ref[...] = total
    far = lax.axis_index("los") // g.plane
    plane = lax.broadcasted_iota(jnp.int32, (g.slab, g.deep), 0) // g.cols
    out_ref[g.column :, :] = jnp.zeros((SUB, g.deep), jnp.float32)
    for i, ref in enumerate(part_refs):
        there = g.far_peer(far, i)
        at = pl.ds(pl.multiple_of(there * g.slab, SUB), g.slab)
        start = g.column + 2 * g.slab
        exponent = picked(jnp.broadcast_to(ref[start : start + 1, :], (g.slab, g.deep)), plane)
        selection = ref[g.column : g.column + g.slab, :]
        counts = ref[g.column + g.slab : start, :]
        out_ref[at, :] = cotangent_of(sum_ref[at, :], selection, counts, exponent)
        out_ref[pl.ds(g.column + there, 1), :] = ref[start + 1 : start + 2, :]


def joined_kernel(*refs):
    rows = refs[0].shape[0]
    for i, ref in enumerate(refs[:-1]):
        at = i * rows
        refs[-1][at : at + rows, :] = ref[...]


def picked(rows, index):
    return jnp.take_along_axis(rows, index, axis=1, mode="promise_in_bounds")


def ready_kernel(g, cell_ref, frac_ref, offset_ref, *refs):
    far_refs, near_refs = refs[:6], refs[11:-1]
    index_ref, weight_ref, info_ref, red_ref, table_ref = refs[6:11]
    copies = started(far_refs, near_refs, refs[-1])
    for copy in copies:
        copy.wait()
    dest_ref, count_ref = near_refs[:2]
    write_table(g, near_refs[2:], table_ref)
    plane_iota, sky_iota = row_iotas(g.cols)
    lane = lax.broadcasted_iota(jnp.int32, (SUB, g.block), 1)
    for k in range(g.blocks):
        offset = jnp.broadcast_to(offset_ref[k : k + 1, :], (SUB, g.block))
        live = lane < count_ref[k]
        info_ref[k : k + 1, :] = jnp.full((1, g.deep), dest_ref[k], jnp.int32)
        red = red_of(g, block_rows(cell_ref, 0, k, g.block), offset)
        sky = block_rows(cell_ref, 1, k, g.block)
        sky_next = jnp.where(sky + 1 == g.sky_wrap, 0, sky + 1)
        deep = block_rows(cell_ref, 2, k, g.block)
        frac_los = block_rows(frac_ref, 0, k, g.block)
        frac_sky = block_rows(frac_ref, 1, k, g.block)
        at_sky, at_next = (sky_iota == sky) & live, (sky_iota == sky_next) & live
        on_sky = jnp.where(at_sky, 1.0 - frac_sky, jnp.where(at_next, frac_sky, 0.0))
        slope_sky = jnp.where(at_next, 1.0, 0.0) - jnp.where(at_sky, 1.0, 0.0)
        frac_deep = block_rows(frac_ref, 2, k, g.block)
        deep_next = jnp.where(deep + 1 == g.deep, 0, deep + 1)
        tiles = [on_sky, slope_sky, frac_deep]
        for i in range(g.tiles):
            plane = plane_iota + i * g.planes_per_tile - red
            tiles.append(jnp.where(plane == 0, 1.0 - frac_los, jnp.where(plane == 1, frac_los, 0.0)))
            tiles.append(jnp.where(plane == 1, 1.0, jnp.where(plane == 0, -1.0, 0.0)))
        index_ref[k, 0] = deep
        index_ref[k, 1] = deep_next
        if g.twice:
            first, top = plane_iota == 0, red == g.slab_rows - 1
            slope_top = jnp.where(top, jnp.where(first, 1.0 - frac_deep, frac_deep), 0.0)
            tiles.append(frac_los * slope_top)
            tiles.append(jnp.where(top, jnp.where(first, -frac_los, frac_los), 0.0))
            tiles.append(slope_top)
            index_ref[k, 2] = jnp.where(first, deep, deep_next)
        for j, tile in enumerate(tiles):
            weight_ref[k, j] = tile
        red_ref[k : k + 1, :] = red[0:1]


def crossed(mask, first, second, distance):
    return jnp.where(mask, first, second) + pltpu.roll(jnp.where(mask, second, first), distance, 0)


def pull_kernel(g, info_ref, index_ref, weight_ref, red_ref, *refs):
    field_refs, (pos_ref, vel_ref, whole_ref, top_ref, rate_ref, own_rate_ref) = refs[:-6], refs[-6:]
    me = lax.axis_index("los")
    tall = g.column + SUB
    for near in range(g.plane):
        ref, base = field_refs[near % 2], (near // 2) * tall
        for far in range(g.planes):
            slab = slab_at(g, me, near, far)
            at = pl.ds(pl.multiple_of(slab * g.slab, SUB), g.slab)
            start = base + far * g.slab
            whole_ref[at, :] = ref[start : start + g.slab, :]
            if g.twice:
                under = pl.multiple_of(lax.rem(slab + g.slabs - 1, g.slabs) * SUB, SUB)
                rows = ref[start : start + g.cols, :]
                top_ref[pl.ds(under, SUB), :] = jnp.concatenate([rows, rows], axis=0)
            start = base + g.column + far
            rate_ref[pl.ds(slab, 1), :] = ref[start : start + 1, :]
    spill = g.window - g.slab
    whole_ref[g.slabs * g.slab :, :] = whole_ref[:spill, :]
    sub = lax.broadcasted_iota(jnp.int32, (SUB, g.block), 0)
    in_even, in_first = sub % 2 == 0, sub % 4 < 2
    for k in range(g.blocks):
        slab = dest_of(info_ref, k)
        deep, deep_next = index_ref[k, 0], index_ref[k, 1]
        on_sky, slope_sky, frac_deep = weight_ref[k, 0], weight_ref[k, 1], weight_ref[k, 2]
        sum_val, sum_los, sum_deep = 0.0, 0.0, 0.0
        for i in range(g.tiles):
            at = pl.ds(pl.multiple_of(slab * g.slab, SUB) + i * SUB, SUB)
            rows = whole_ref[at, :]
            below = picked(rows, deep)
            step = picked(rows, deep_next) - below
            value = below + frac_deep * step
            on_los, slope_los = weight_ref[k, 3 + 2 * i], weight_ref[k, 4 + 2 * i]
            sum_val += on_los * value
            sum_deep += on_los * step
            sum_los += slope_los * value
        if g.twice:
            rows = picked(top_ref[pl.ds(pl.multiple_of(slab * SUB, SUB), SUB), :], index_ref[k, 2])
            sum_val += weight_ref[k, 3 + 2 * g.tiles] * rows
            sum_deep += weight_ref[k, 4 + 2 * g.tiles] * rows
            sum_los += weight_ref[k, 5 + 2 * g.tiles] * rows
        lanes = slice(k * g.block, (k + 1) * g.block)
        own_rate_ref[k : k + 1, :] = rate_ref[pl.ds(slab, 1), :]
        pair = crossed(in_even, on_sky * sum_los, slope_sky * sum_val, 1)
        other = on_sky * sum_deep
        four = crossed(in_first, pair, other + pltpu.roll(other, 1, 0), 2)
        grads = four + pltpu.roll(four, 4, 0)
        pos_ref[:, lanes] = grads[:3]
        vel_ref[k : k + 1, :] = grads[0:1]
    for k in range(0, g.blocks, SUB):
        rows = slice(k, k + SUB)
        vel_ref[rows, :] = vel_ref[rows, :] * picked(own_rate_ref[rows, :], red_ref[rows, :])


class Geometry:
    def __init__(self, slabs, sky_parts, cell_shape, block_shape, field_shape):
        self.slabs = slabs
        self.blocks = block_shape[0]
        self.block = cell_shape[1] // self.blocks
        self.slab_rows, self.width, self.deep = field_shape
        self.sky_wrap = self.width if sky_parts == 1 else -1
        need = self.width + (sky_parts > 1)
        self.cols = next(c for c in (1, 2, 4, 8) if c >= need and c * self.slab_rows % SUB == 0)
        self.planes_per_tile = SUB // self.cols
        self.cell_type = jnp.bfloat16 if self.deep <= 256 else jnp.float32
        self.slab = self.slab_rows * self.cols
        self.plane = 8
        self.planes = slabs // self.plane
        self.column = self.planes * self.slab
        self.window = rounded_up(self.slab + self.cols, SUB)

        self.twice = self.planes_per_tile == 2 and self.slab % SUB == 0
        self.tiles = (self.slab if self.twice else self.window) // SUB

    def far_peer(self, far, m):
        even = self.planes & (self.planes - 1) == 0
        return far ^ m if even else (far + m) % self.planes


def on_device(
    part_cell,
    part_frac,
    los_offset,
    block_dest,
    block_count,
    selection,
    galaxy_counts,
    bias_exp,
    rsd_factor,
):
    sky_parts = lax.axis_size("sky")
    g = Geometry(
        lax.axis_size("los"), sky_parts, part_cell.shape, block_dest.shape, selection.shape
    )
    f32 = jnp.float32
    vmem = pl.BlockSpec(memory_space=pltpu.VMEM)
    if sky_parts > 1:
        shift = jnp.stack([0, lax.axis_index("sky") * g.width, 0]).astype(jnp.int32)
        part_cell = part_cell - shift[:, None]
    offsets = los_offset.reshape(g.blocks, g.block)
    size = g.slabs * g.slab
    padded = size + g.window - g.slab
    small = pltpu.CompilerParams(vmem_limit_bytes=VMEM_LIMIT)

    def tiled(rows):
        return jax.ShapeDtypeStruct((rows, g.deep), f32)

    def to_near(block, near):
        return lax.ppermute(block, "los", [(i ^ near, i) for i in range(g.slabs)])

    def spread(move, blocks):
        return [move(block, j) for j, block in enumerate(blocks, 1)]

    def from_far(block, m):
        rest = [(i // g.plane, i % g.plane) for i in range(g.slabs)]
        route = [(g.far_peer(far, m) * g.plane + near, far * g.plane + near) for far, near in rest]
        return lax.ppermute(block, "los", route)

    def held(*arrays):
        return [pltpu.with_memory_space_constraint(x, pltpu.HBM) for x in arrays]

    far = pl.BlockSpec(memory_space=pltpu.HBM)
    scalars = [
        pltpu.SMEM(block_dest.shape, jnp.int32),
        pltpu.SMEM(block_count.shape, jnp.int32),
    ]
    cell, frac, offset, keep, send = pl.pallas_call(
        functools.partial(paint_kernel, g),
        out_shape=(
            pltpu.VMEM(part_cell.shape, jnp.int32),
            pltpu.VMEM(part_frac.shape, f32),
            pltpu.VMEM(offsets.shape, jnp.int32),
            pltpu.VMEM((size // 2, g.deep), f32),
            pltpu.VMEM((size // 2, g.deep), f32),
        ),
        in_specs=[far] * 5,
        out_specs=(vmem,) * 5,
        scratch_shapes=[
            *scalars,
            pltpu.VMEM((padded, g.deep), f32),
            pltpu.VMEM((padded, g.deep), f32),
            pltpu.SemaphoreType.DMA((5,)),
        ],
        compiler_params=small,
        name="paint",
    )(*held(block_dest, block_count, part_cell, part_frac, offsets))
    tiles = (g.blocks, 3 + 2 * g.tiles + 3 * g.twice, SUB, g.block)
    index, weight, info, red, table = pl.pallas_call(
        functools.partial(ready_kernel, g),
        out_shape=(
            pltpu.VMEM((g.blocks, 3, SUB, g.block), jnp.int32),
            pltpu.VMEM(tiles, f32),
            pltpu.VMEM((g.blocks, g.deep), jnp.int32),
            pltpu.VMEM((g.blocks, g.block), jnp.int32),
            pltpu.VMEM((2 * g.slab + SUB, g.deep), f32),
        ),
        in_specs=[vmem] * 3 + [far] * 6,
        out_specs=(vmem,) * 5,
        scratch_shapes=[
            *scalars,
            pltpu.VMEM(selection.shape, f32),
            pltpu.VMEM(galaxy_counts.shape, jnp.int32),
            pltpu.SMEM(bias_exp.shape, f32),
            pltpu.SMEM(rsd_factor.shape, f32),
            pltpu.SemaphoreType.DMA((6,)),
        ],
        compiler_params=small,
        cost_estimate=pl.CostEstimate(flops=10**6, bytes_accessed=4 * 10**6, transcendentals=0),
        name="ready",
    )(
        cell,
        frac,
        offset,
        *held(block_dest, block_count, selection, galaxy_counts, bias_exp, rsd_factor),
    )
    quarters = g.plane // 2
    pair = (keep + to_near(send, 1)).reshape(quarters, g.column, g.deep)
    column = pl.pallas_call(
        functools.partial(column_kernel, g),
        out_shape=tiled(g.column + 2 * g.slab + SUB),
        in_specs=[vmem] * (quarters + 1),
        out_specs=vmem,
        compiler_params=small,
        name="column",
    )(pair[0], *spread(lambda block, j: to_near(block, 2 * j), list(pair[1:])), table)
    parts = [column] + spread(from_far, [column] * (g.planes - 1))
    tall = g.column + SUB
    if sky_parts == 1:
        field = pl.pallas_call(
            functools.partial(field_kernel, g),
            out_shape=tiled(tall),
            in_specs=[vmem] * g.planes,
            out_specs=vmem,
            scratch_shapes=[pltpu.VMEM((g.column, g.deep), f32)],
            compiler_params=small,
            name="field",
        )(*parts)
    else:
        here = lax.axis_index("los") // g.plane
        stacked = jnp.stack(parts)
        planes = jnp.zeros_like(stacked[:, g.column :])
        for m in range(g.planes):
            planes = lax.dynamic_update_index_in_dim(
                planes, stacked[m, g.column :], g.far_peer(here, m), 0
            )
        cells = planes[:, : 2 * g.slab].reshape(g.planes, 2, g.slab_rows, g.cols, g.deep)
        power = planes[:, 2 * g.slab, : g.slab_rows, None, None]
        core = jnp.sum(stacked[:, : g.column], axis=0)
        core = core.reshape(g.planes, g.slab_rows, g.cols, g.deep)
        edge = passed_along(core[:, :, g.width], "sky", 1)
        density = core[:, :, : g.width].at[:, :, 0].add(edge)
        near = cells[:, :, :, : g.width]
        inner = cotangent_of(density, near[:, 0], near[:, 1], power)
        rim = passed_along(inner[:, :, 0], "sky", -1)
        rest = jnp.zeros((g.planes, g.slab_rows, g.cols - g.width - 1, g.deep), f32)
        inner = jnp.concatenate([inner, rim[:, :, None], rest], axis=2).reshape(g.column, g.deep)
        rates = jnp.pad(planes[:, 2 * g.slab + 1], ((0, SUB - g.planes), (0, 0)))
        field = jnp.concatenate([inner, rates])
    even = pl.pallas_call(
        joined_kernel,
        out_shape=tiled(quarters * tall),
        in_specs=[vmem] * quarters,
        out_specs=vmem,
        compiler_params=small,
        name="joined",
    )(field, *spread(lambda block, j: to_near(block, 2 * j), [field] * (quarters - 1)))
    fields = [even, to_near(even, 1)]
    grad_pos, grad_vel = pl.pallas_call(
        functools.partial(pull_kernel, g),
        out_shape=(
            jax.ShapeDtypeStruct(part_frac.shape, f32),
            jax.ShapeDtypeStruct((g.blocks, g.block), f32),
        ),
        in_specs=[vmem] * 6,
        out_specs=(vmem, vmem),
        scratch_shapes=[
            pltpu.VMEM((padded, g.deep), f32),
            pltpu.VMEM((g.slabs * SUB, g.deep), f32),
            pltpu.VMEM((g.slabs, g.deep), f32),
            pltpu.VMEM((g.blocks, g.deep), f32),
        ],
        compiler_params=small,
        name="pull",
    )(info, index, weight, red, *fields)
    return grad_pos, grad_vel.reshape(-1)


def solution(mesh):
    return jax.shard_map(
        on_device,
        mesh=mesh,
        in_specs=(
            P(None, ("los", "sky")),
            P(None, ("los", "sky")),
            P(("los", "sky")),
            P(("los", "sky")),
            P(("los", "sky")),
            P("los", "sky", None),
            P("los", "sky", None),
            P("los"),
            P("los"),
        ),
        out_specs=(P(None, ("los", "sky")), P(("los", "sky"))),
        check_vma=False,
    )
```

```python
import functools

import jax
import jax.numpy as jnp
from jax import lax
from jax.experimental import pallas as pl
from jax.experimental.pallas import tpu as pltpu
from jax.sharding import PartitionSpec as P

SUB = 8
VMEM_LIMIT = 8 * 1024 * 1024


def passed_along(block, axis, distance):
    devices = range(lax.axis_size(axis))
    route = [((i - distance) % len(devices), i) for i in devices]
    return lax.ppermute(block, axis, route)


def rounded_up(value, step):
    return -(-value // step) * step


def row_iotas(cols):
    sub = lax.broadcasted_iota(jnp.int32, (SUB, 128), 0)
    return sub // cols, sub % cols


def block_rows(ref, row, k, lanes):
    return jnp.broadcast_to(ref[row : row + 1, k * lanes : (k + 1) * lanes], (SUB, lanes))


def slab_at(g, me, near, far):
    return far * g.plane + ((me % g.plane) ^ near)


def write_table(g, refs, table_ref):
    selection_ref, counts_ref, bias_ref, rate_ref = refs
    sub = lax.broadcasted_iota(jnp.int32, (SUB, g.deep), 0)
    lane = lax.broadcasted_iota(jnp.int32, (SUB, g.deep), 1)
    rest = jnp.zeros((SUB, g.deep), jnp.float32)
    table_ref[...] = jnp.zeros_like(table_ref)
    for j in range(g.slab_rows):
        rest = jnp.where(lane == j, jnp.where(sub == 0, bias_ref[j], rate_ref[j]), rest)
        start = j * g.cols
        table_ref[start : start + g.width, :] = selection_ref[j]
        table_ref[g.slab + start : g.slab + start + g.width, :] = counts_ref[j].astype(jnp.float32)
    table_ref[2 * g.slab :, :] = rest


def started(sources, targets, arrived):
    copies = [
        pltpu.make_async_copy(a, b, arrived.at[i])
        for i, (a, b) in enumerate(zip(sources, targets, strict=True))
    ]
    for copy in copies:
        copy.start()
    return copies


def dest_of(dest_ref, k):
    return dest_ref[k : k + 1, 0:1][0, 0]


def red_of(g, cell, offset):
    even = g.slab_rows & (g.slab_rows - 1) == 0
    return (cell + offset) & (g.slab_rows - 1) if even else jnp.mod(cell + offset, g.slab_rows)


def paint_kernel(g, *refs):
    far_refs, (cell_ref, frac_ref, offset_ref, keep_ref, send_ref), refs = refs[:5], refs[5:10], refs[10:]
    dest_ref, count_ref, sum_ref, turn_ref, arrived = refs
    copies = started(far_refs, (dest_ref, count_ref, cell_ref, frac_ref, offset_ref), arrived)
    sum_ref[...] = jnp.zeros_like(sum_ref)
    lane = lax.broadcasted_iota(jnp.int32, (SUB, g.block), 1)
    plane_iota, sky_iota = row_iotas(g.cols)
    deep_iota = lax.broadcasted_iota(jnp.int32, (g.block, g.deep), 1)
    under_iota = jnp.where(deep_iota == 0, g.deep - 1, deep_iota - 1)
    cell_type = jnp.bfloat16 if g.deep <= 256 else jnp.float32
    both_iota = jnp.concatenate([deep_iota, under_iota], axis=0).astype(jnp.float32).astype(cell_type)
    one, zero = jnp.ones_like(both_iota), jnp.zeros_like(both_iota)
    for copy in copies[2:]:
        copy.wait()
    for k in range(g.blocks):
        turn_ref[k : k + 1, :] = cell_ref[2:3, k * g.block : (k + 1) * g.block].astype(jnp.float32)
    turned = turn_ref[...].T
    for copy in copies[:2]:
        copy.wait()
    for k in range(g.blocks):
        offset = jnp.broadcast_to(offset_ref[k : k + 1, :], (SUB, g.block))
        red = red_of(g, block_rows(cell_ref, 0, k, g.block), offset)
        sky = block_rows(cell_ref, 1, k, g.block)
        sky_next = jnp.where(sky + 1 == g.sky_wrap, 0, sky + 1)
        frac_los = block_rows(frac_ref, 0, k, g.block)
        frac_sky = block_rows(frac_ref, 1, k, g.block)
        frac_deep = block_rows(frac_ref, 2, k, g.block)
        on_sky = jnp.where(
            sky_iota == sky, 1.0 - frac_sky, jnp.where(sky_iota == sky_next, frac_sky, 0.0)
        )
        on_sky = jnp.where(lane < count_ref[k], on_sky, 0.0)
        rows = []
        for i in range(g.window // SUB):
            plane = plane_iota + i * g.planes_per_tile - red
            on_los = jnp.where(
                plane == 0, 1.0 - frac_los, jnp.where(plane == 1, frac_los, 0.0)
            )
            rows.append(on_los * on_sky)
        weight = jnp.concatenate(rows, axis=0)
        upper = weight * jnp.concatenate([frac_deep] * (g.window // SUB), axis=0)
        weight = jnp.concatenate([weight - upper, upper], axis=1)
        coarse = weight.astype(jnp.bfloat16).astype(jnp.float32)
        split = jnp.concatenate([coarse, weight - coarse], axis=0).astype(jnp.bfloat16)
        deep = jnp.broadcast_to(turned[:, k : k + 1], (g.block, g.deep)).astype(cell_type)
        hit = jnp.where(both_iota == jnp.concatenate([deep, deep], axis=0), one, zero)
        got = jnp.dot(
            split,
            hit.astype(jnp.bfloat16),
            preferred_element_type=jnp.float32,
        )
        at = pl.ds(pl.multiple_of(dest_ref[k] * g.slab, SUB), g.window)
        sum_ref[at, :] += got[: g.window] + got[g.window :]
    size = g.slabs * g.slab
    spill = g.window - g.slab
    sum_ref[:spill, :] += sum_ref[size:, :]
    me = lax.axis_index("los")
    for near in range(g.plane):
        for far in range(g.planes):
            at = pl.ds(pl.multiple_of(slab_at(g, me, near, far) * g.slab, SUB), g.slab)
            start = (near // 2) * g.column + far * g.slab
            (send_ref if near % 2 else keep_ref)[start : start + g.slab, :] = sum_ref[at, :]


def cotangent_of(density, selection, counts, exponent):
    shifted = density + 0.5
    intensity = selection * jnp.exp(exponent * jnp.log(shifted))
    return (1.0 - counts.astype(jnp.float32) / intensity) * exponent * intensity / shifted


def column_kernel(g, own_ref, *refs):
    total = own_ref[...]
    for ref in refs[:-2]:
        total = total + ref[...]
    refs[-1][: g.column, :] = total
    refs[-1][g.column :, :] = refs[-2][...]


def field_kernel(g, *refs):
    part_refs, out_ref, sum_ref = refs[: g.planes], refs[-2], refs[-1]
    total = part_refs[0][: g.column, :]
    for ref in part_refs[1:]:
        total = total + ref[: g.column, :]
    sum_ref[...] = total
    far = lax.axis_index("los") // g.plane
    plane = lax.broadcasted_iota(jnp.int32, (g.slab, g.deep), 0) // g.cols
    out_ref[g.column :, :] = jnp.zeros((SUB, g.deep), jnp.float32)
    for i, ref in enumerate(part_refs):
        there = g.far_peer(far, i)
        at = pl.ds(pl.multiple_of(there * g.slab, SUB), g.slab)
        start = g.column + 2 * g.slab
        exponent = picked(jnp.broadcast_to(ref[start : start + 1, :], (g.slab, g.deep)), plane)
        selection = ref[g.column : g.column + g.slab, :]
        counts = ref[g.column + g.slab : start, :]
        out_ref[at, :] = cotangent_of(sum_ref[at, :], selection, counts, exponent)
        out_ref[pl.ds(g.column + there, 1), :] = ref[start + 1 : start + 2, :]


def joined_kernel(*refs):
    rows = refs[0].shape[0]
    for i, ref in enumerate(refs[:-1]):
        at = i * rows
        refs[-1][at : at + rows, :] = ref[...]


def picked(rows, index):
    return jnp.take_along_axis(rows, index, axis=1, mode="promise_in_bounds")


def ready_kernel(g, cell_ref, frac_ref, offset_ref, *refs):
    far_refs, near_refs = refs[:6], refs[11:-1]
    index_ref, weight_ref, info_ref, red_ref, table_ref = refs[6:11]
    copies = started(far_refs, near_refs, refs[-1])
    for copy in copies:
        copy.wait()
    dest_ref, count_ref = near_refs[:2]
    write_table(g, near_refs[2:], table_ref)
    plane_iota, sky_iota = row_iotas(g.cols)
    lane = lax.broadcasted_iota(jnp.int32, (SUB, g.block), 1)
    for k in range(g.blocks):
        offset = jnp.broadcast_to(offset_ref[k : k + 1, :], (SUB, g.block))
        live = lane < count_ref[k]
        info_ref[k : k + 1, :] = jnp.full((1, g.deep), dest_ref[k], jnp.int32)
        red = red_of(g, block_rows(cell_ref, 0, k, g.block), offset)
        sky = block_rows(cell_ref, 1, k, g.block)
        sky_next = jnp.where(sky + 1 == g.sky_wrap, 0, sky + 1)
        deep = block_rows(cell_ref, 2, k, g.block)
        frac_los = block_rows(frac_ref, 0, k, g.block)
        frac_sky = block_rows(frac_ref, 1, k, g.block)
        at_sky, at_next = (sky_iota == sky) & live, (sky_iota == sky_next) & live
        on_sky = jnp.where(at_sky, 1.0 - frac_sky, jnp.where(at_next, frac_sky, 0.0))
        slope_sky = jnp.where(at_next, 1.0, 0.0) - jnp.where(at_sky, 1.0, 0.0)
        frac_deep = block_rows(frac_ref, 2, k, g.block)
        deep_next = jnp.where(deep + 1 == g.deep, 0, deep + 1)
        tiles = [on_sky, slope_sky, frac_deep]
        for i in range(g.tiles):
            plane = plane_iota + i * g.planes_per_tile - red
            tiles.append(jnp.where(plane == 0, 1.0 - frac_los, jnp.where(plane == 1, frac_los, 0.0)))
            tiles.append(jnp.where(plane == 1, 1.0, jnp.where(plane == 0, -1.0, 0.0)))
        index_ref[k, 0] = deep
        index_ref[k, 1] = deep_next
        if g.twice:
            first, top = plane_iota == 0, red == g.slab_rows - 1
            slope_top = jnp.where(top, jnp.where(first, 1.0 - frac_deep, frac_deep), 0.0)
            tiles.append(frac_los * slope_top)
            tiles.append(jnp.where(top, jnp.where(first, -frac_los, frac_los), 0.0))
            tiles.append(slope_top)
            index_ref[k, 2] = jnp.where(first, deep, deep_next)
        for j, tile in enumerate(tiles):
            weight_ref[k, j] = tile
        red_ref[k : k + 1, :] = red[0:1]


def crossed(mask, first, second, distance):
    return jnp.where(mask, first, second) + pltpu.roll(jnp.where(mask, second, first), distance, 0)


def pull_kernel(g, info_ref, index_ref, weight_ref, red_ref, *refs):
    field_refs, (pos_ref, vel_ref, whole_ref, top_ref, rate_ref, own_rate_ref) = refs[:-6], refs[-6:]
    me = lax.axis_index("los")
    tall = g.column + SUB
    for near in range(g.plane):
        ref, base = field_refs[near % 2], (near // 2) * tall
        for far in range(g.planes):
            slab = slab_at(g, me, near, far)
            at = pl.ds(pl.multiple_of(slab * g.slab, SUB), g.slab)
            start = base + far * g.slab
            whole_ref[at, :] = ref[start : start + g.slab, :]
            if g.twice:
                under = pl.multiple_of(lax.rem(slab + g.slabs - 1, g.slabs) * SUB, SUB)
                rows = ref[start : start + g.cols, :]
                top_ref[pl.ds(under, SUB), :] = jnp.concatenate([rows, rows], axis=0)
            start = base + g.column + far
            rate_ref[pl.ds(slab, 1), :] = ref[start : start + 1, :]
    spill = g.window - g.slab
    whole_ref[g.slabs * g.slab :, :] = whole_ref[:spill, :]
    sub = lax.broadcasted_iota(jnp.int32, (SUB, g.block), 0)
    in_even, in_first = sub % 2 == 0, sub % 4 < 2
    for k in range(g.blocks):
        slab = dest_of(info_ref, k)
        deep, deep_next = index_ref[k, 0], index_ref[k, 1]
        on_sky, slope_sky, frac_deep = weight_ref[k, 0], weight_ref[k, 1], weight_ref[k, 2]
        sum_val, sum_los, sum_deep = 0.0, 0.0, 0.0
        for i in range(g.tiles):
            at = pl.ds(pl.multiple_of(slab * g.slab, SUB) + i * SUB, SUB)
            rows = whole_ref[at, :]
            below = picked(rows, deep)
            step = picked(rows, deep_next) - below
            value = below + frac_deep * step
            on_los, slope_los = weight_ref[k, 3 + 2 * i], weight_ref[k, 4 + 2 * i]
            sum_val += on_los * value
            sum_deep += on_los * step
            sum_los += slope_los * value
        if g.twice:
            rows = picked(top_ref[pl.ds(pl.multiple_of(slab * SUB, SUB), SUB), :], index_ref[k, 2])
            sum_val += weight_ref[k, 3 + 2 * g.tiles] * rows
            sum_deep += weight_ref[k, 4 + 2 * g.tiles] * rows
            sum_los += weight_ref[k, 5 + 2 * g.tiles] * rows
        lanes = slice(k * g.block, (k + 1) * g.block)
        own_rate_ref[k : k + 1, :] = rate_ref[pl.ds(slab, 1), :]
        pair = crossed(in_even, on_sky * sum_los, slope_sky * sum_val, 1)
        other = on_sky * sum_deep
        four = crossed(in_first, pair, other + pltpu.roll(other, 1, 0), 2)
        grads = four + pltpu.roll(four, 4, 0)
        pos_ref[:, lanes] = grads[:3]
        vel_ref[k : k + 1, :] = grads[0:1]
    for k in range(0, g.blocks, SUB):
        rows = slice(k, k + SUB)
        vel_ref[rows, :] = vel_ref[rows, :] * picked(own_rate_ref[rows, :], red_ref[rows, :])


class Geometry:
    def __init__(self, slabs, sky_parts, cell_shape, block_shape, field_shape):
        self.slabs = slabs
        self.blocks = block_shape[0]
        self.block = cell_shape[1] // self.blocks
        self.slab_rows, self.width, self.deep = field_shape
        self.sky_wrap = self.width if sky_parts == 1 else -1
        need = self.width + (sky_parts > 1)
        self.cols = next(c for c in (1, 2, 4, 8) if c >= need and c * self.slab_rows % SUB == 0)
        self.planes_per_tile = SUB // self.cols
        self.slab = self.slab_rows * self.cols
        self.plane = 8
        self.planes = slabs // self.plane
        self.column = self.planes * self.slab
        self.window = rounded_up(self.slab + self.cols, SUB)

        self.twice = self.planes_per_tile == 2 and self.slab % SUB == 0
        self.tiles = (self.slab if self.twice else self.window) // SUB

    def far_peer(self, far, m):
        even = self.planes & (self.planes - 1) == 0
        return far ^ m if even else (far + m) % self.planes


def on_device(
    part_cell,
    part_frac,
    los_offset,
    block_dest,
    block_count,
    selection,
    galaxy_counts,
    bias_exp,
    rsd_factor,
):
    sky_parts = lax.axis_size("sky")
    g = Geometry(
        lax.axis_size("los"), sky_parts, part_cell.shape, block_dest.shape, selection.shape
    )
    f32 = jnp.float32
    vmem = pl.BlockSpec(memory_space=pltpu.VMEM)
    if sky_parts > 1:
        shift = jnp.stack([0, lax.axis_index("sky") * g.width, 0]).astype(jnp.int32)
        part_cell = part_cell - shift[:, None]
    offsets = los_offset.reshape(g.blocks, g.block)
    size = g.slabs * g.slab
    padded = size + g.window - g.slab
    small = pltpu.CompilerParams(vmem_limit_bytes=VMEM_LIMIT)

    def tiled(rows):
        return jax.ShapeDtypeStruct((rows, g.deep), f32)

    def to_near(block, near):
        return lax.ppermute(block, "los", [(i ^ near, i) for i in range(g.slabs)])

    def spread(move, blocks):
        return [move(block, j) for j, block in enumerate(blocks, 1)]

    def from_far(block, m):
        rest = [(i // g.plane, i % g.plane) for i in range(g.slabs)]
        route = [(g.far_peer(far, m) * g.plane + near, far * g.plane + near) for far, near in rest]
        return lax.ppermute(block, "los", route)

    def held(*arrays):
        return [pltpu.with_memory_space_constraint(x, pltpu.HBM) for x in arrays]

    far = pl.BlockSpec(memory_space=pltpu.HBM)
    scalars = [
        pltpu.SMEM(block_dest.shape, jnp.int32),
        pltpu.SMEM(block_count.shape, jnp.int32),
    ]
    cell, frac, offset, keep, send = pl.pallas_call(
        functools.partial(paint_kernel, g),
        out_shape=(
            pltpu.VMEM(part_cell.shape, jnp.int32),
            pltpu.VMEM(part_frac.shape, f32),
            pltpu.VMEM(offsets.shape, jnp.int32),
            pltpu.VMEM((size // 2, g.deep), f32),
            pltpu.VMEM((size // 2, g.deep), f32),
        ),
        in_specs=[far] * 5,
        out_specs=(vmem,) * 5,
        scratch_shapes=[
            *scalars,
            pltpu.VMEM((padded, g.deep), f32),
            pltpu.VMEM((rounded_up(g.blocks, SUB), g.block), f32),
            pltpu.SemaphoreType.DMA((5,)),
        ],
        compiler_params=small,
        name="paint",
    )(*held(block_dest, block_count, part_cell, part_frac, offsets))
    tiles = (g.blocks, 3 + 2 * g.tiles + 3 * g.twice, SUB, g.block)
    index, weight, info, red, table = pl.pallas_call(
        functools.partial(ready_kernel, g),
        out_shape=(
            pltpu.VMEM((g.blocks, 3, SUB, g.block), jnp.int32),
            pltpu.VMEM(tiles, f32),
            pltpu.VMEM((g.blocks, g.deep), jnp.int32),
            pltpu.VMEM((g.blocks, g.block), jnp.int32),
            pltpu.VMEM((2 * g.slab + SUB, g.deep), f32),
        ),
        in_specs=[vmem] * 3 + [far] * 6,
        out_specs=(vmem,) * 5,
        scratch_shapes=[
            *scalars,
            pltpu.VMEM(selection.shape, f32),
            pltpu.VMEM(galaxy_counts.shape, jnp.int32),
            pltpu.SMEM(bias_exp.shape, f32),
            pltpu.SMEM(rsd_factor.shape, f32),
            pltpu.SemaphoreType.DMA((6,)),
        ],
        compiler_params=small,
        cost_estimate=pl.CostEstimate(flops=10**6, bytes_accessed=4 * 10**6, transcendentals=0),
        name="ready",
    )(
        cell,
        frac,
        offset,
        *held(block_dest, block_count, selection, galaxy_counts, bias_exp, rsd_factor),
    )
    quarters = g.plane // 2
    pair = (keep + to_near(send, 1)).reshape(quarters, g.column, g.deep)
    column = pl.pallas_call(
        functools.partial(column_kernel, g),
        out_shape=tiled(g.column + 2 * g.slab + SUB),
        in_specs=[vmem] * (quarters + 1),
        out_specs=vmem,
        compiler_params=small,
        name="column",
    )(pair[0], *spread(lambda block, j: to_near(block, 2 * j), list(pair[1:])), table)
    parts = [column] + spread(from_far, [column] * (g.planes - 1))
    tall = g.column + SUB
    if sky_parts == 1:
        field = pl.pallas_call(
            functools.partial(field_kernel, g),
            out_shape=tiled(tall),
            in_specs=[vmem] * g.planes,
            out_specs=vmem,
            scratch_shapes=[pltpu.VMEM((g.column, g.deep), f32)],
            compiler_params=small,
            name="field",
        )(*parts)
    else:
        here = lax.axis_index("los") // g.plane
        stacked = jnp.stack(parts)
        planes = jnp.zeros_like(stacked[:, g.column :])
        for m in range(g.planes):
            planes = lax.dynamic_update_index_in_dim(
                planes, stacked[m, g.column :], g.far_peer(here, m), 0
            )
        cells = planes[:, : 2 * g.slab].reshape(g.planes, 2, g.slab_rows, g.cols, g.deep)
        power = planes[:, 2 * g.slab, : g.slab_rows, None, None]
        core = jnp.sum(stacked[:, : g.column], axis=0)
        core = core.reshape(g.planes, g.slab_rows, g.cols, g.deep)
        edge = passed_along(core[:, :, g.width], "sky", 1)
        density = core[:, :, : g.width].at[:, :, 0].add(edge)
        near = cells[:, :, :, : g.width]
        inner = cotangent_of(density, near[:, 0], near[:, 1], power)
        rim = passed_along(inner[:, :, 0], "sky", -1)
        rest = jnp.zeros((g.planes, g.slab_rows, g.cols - g.width - 1, g.deep), f32)
        inner = jnp.concatenate([inner, rim[:, :, None], rest], axis=2).reshape(g.column, g.deep)
        rates = jnp.pad(planes[:, 2 * g.slab + 1], ((0, SUB - g.planes), (0, 0)))
        field = jnp.concatenate([inner, rates])
    even = pl.pallas_call(
        joined_kernel,
        out_shape=tiled(quarters * tall),
        in_specs=[vmem] * quarters,
        out_specs=vmem,
        compiler_params=small,
        name="joined",
    )(field, *spread(lambda block, j: to_near(block, 2 * j), [field] * (quarters - 1)))
    fields = [even, to_near(even, 1)]
    grad_pos, grad_vel = pl.pallas_call(
        functools.partial(pull_kernel, g),
        out_shape=(
            jax.ShapeDtypeStruct(part_frac.shape, f32),
            jax.ShapeDtypeStruct((g.blocks, g.block), f32),
        ),
        in_specs=[vmem] * 6,
        out_specs=(vmem, vmem),
        scratch_shapes=[
            pltpu.VMEM((padded, g.deep), f32),
            pltpu.VMEM((g.slabs * SUB, g.deep), f32),
            pltpu.VMEM((g.slabs, g.deep), f32),
            pltpu.VMEM((g.blocks, g.deep), f32),
        ],
        compiler_params=small,
        name="pull",
    )(info, index, weight, red, *fields)
    return grad_pos, grad_vel.reshape(-1)


def solution(mesh):
    return jax.shard_map(
        on_device,
        mesh=mesh,
        in_specs=(
            P(None, ("los", "sky")),
            P(None, ("los", "sky")),
            P(("los", "sky")),
            P(("los", "sky")),
            P(("los", "sky")),
            P("los", "sky", None),
            P("los", "sky", None),
            P("los"),
            P("los"),
        ),
        out_specs=(P(None, ("los", "sky")), P(("los", "sky"))),
        check_vma=False,
    )
```

```python
import functools

import jax
import jax.numpy as jnp
from jax import lax
from jax.experimental import pallas as pl
from jax.experimental.pallas import tpu as pltpu
from jax.sharding import PartitionSpec as P

SUB = 8
VMEM_LIMIT = 8 * 1024 * 1024


def passed_along(block, axis, distance):
    devices = range(lax.axis_size(axis))
    route = [((i - distance) % len(devices), i) for i in devices]
    return lax.ppermute(block, axis, route)


def rounded_up(value, step):
    return -(-value // step) * step


def row_iotas(cols):
    sub = lax.broadcasted_iota(jnp.int32, (SUB, 128), 0)
    return sub // cols, sub % cols


def block_rows(ref, row, k, lanes):
    return jnp.broadcast_to(ref[row : row + 1, k * lanes : (k + 1) * lanes], (SUB, lanes))


def slab_at(g, me, near, far):
    return far * g.plane + ((me % g.plane) ^ near)


def write_table(g, refs, table_ref):
    selection_ref, counts_ref, bias_ref, rate_ref = refs
    sub = lax.broadcasted_iota(jnp.int32, (SUB, g.deep), 0)
    lane = lax.broadcasted_iota(jnp.int32, (SUB, g.deep), 1)
    rest = jnp.zeros((SUB, g.deep), jnp.float32)
    table_ref[...] = jnp.zeros_like(table_ref)
    for j in range(g.slab_rows):
        rest = jnp.where(lane == j, jnp.where(sub == 0, bias_ref[j], rate_ref[j]), rest)
        start = j * g.cols
        table_ref[start : start + g.width, :] = selection_ref[j]
        table_ref[g.slab + start : g.slab + start + g.width, :] = counts_ref[j].astype(jnp.float32)
    table_ref[2 * g.slab :, :] = rest


def started(sources, targets, arrived):
    copies = [
        pltpu.make_async_copy(a, b, arrived.at[i])
        for i, (a, b) in enumerate(zip(sources, targets, strict=True))
    ]
    for copy in copies:
        copy.start()
    return copies


def dest_of(dest_ref, k):
    return dest_ref[k : k + 1, 0:1][0, 0]


def red_of(g, cell, offset):
    even = g.slab_rows & (g.slab_rows - 1) == 0
    return (cell + offset) & (g.slab_rows - 1) if even else jnp.mod(cell + offset, g.slab_rows)


def paint_kernel(g, *refs):
    far_refs, (cell_ref, frac_ref, offset_ref), part_refs, refs = refs[:5], refs[5:8], refs[8:12], refs[12:]
    dest_ref, count_ref, sum_ref, turn_ref, arrived = refs
    copies = started(far_refs, (dest_ref, count_ref, cell_ref, frac_ref, offset_ref), arrived)
    sum_ref[...] = jnp.zeros_like(sum_ref)
    lane = lax.broadcasted_iota(jnp.int32, (SUB, g.block), 1)
    plane_iota, sky_iota = row_iotas(g.cols)
    deep_iota = lax.broadcasted_iota(jnp.int32, (g.block, g.deep), 1)
    under_iota = jnp.where(deep_iota == 0, g.deep - 1, deep_iota - 1)
    cell_type = jnp.bfloat16 if g.deep <= 256 else jnp.float32
    both_iota = jnp.concatenate([deep_iota, under_iota], axis=0).astype(jnp.float32).astype(cell_type)
    one, zero = jnp.ones_like(both_iota), jnp.zeros_like(both_iota)
    for copy in copies[2:]:
        copy.wait()
    for k in range(g.blocks):
        turn_ref[k : k + 1, :] = cell_ref[2:3, k * g.block : (k + 1) * g.block].astype(jnp.float32)
    turned = turn_ref[...].T
    for copy in copies[:2]:
        copy.wait()
    for k in range(g.blocks):
        offset = jnp.broadcast_to(offset_ref[k : k + 1, :], (SUB, g.block))
        red = red_of(g, block_rows(cell_ref, 0, k, g.block), offset)
        sky = block_rows(cell_ref, 1, k, g.block)
        sky_next = jnp.where(sky + 1 == g.sky_wrap, 0, sky + 1)
        frac_los = block_rows(frac_ref, 0, k, g.block)
        frac_sky = block_rows(frac_ref, 1, k, g.block)
        frac_deep = block_rows(frac_ref, 2, k, g.block)
        on_sky = jnp.where(
            sky_iota == sky, 1.0 - frac_sky, jnp.where(sky_iota == sky_next, frac_sky, 0.0)
        )
        on_sky = jnp.where(lane < count_ref[k], on_sky, 0.0)
        rows = []
        for i in range(g.window // SUB):
            plane = plane_iota + i * g.planes_per_tile - red
            on_los = jnp.where(
                plane == 0, 1.0 - frac_los, jnp.where(plane == 1, frac_los, 0.0)
            )
            rows.append(on_los * on_sky)
        weight = jnp.concatenate(rows, axis=0)
        upper = weight * jnp.concatenate([frac_deep] * (g.window // SUB), axis=0)
        weight = jnp.concatenate([weight - upper, upper], axis=1)
        coarse = weight.astype(jnp.bfloat16).astype(jnp.float32)
        split = jnp.concatenate([coarse, weight - coarse], axis=0).astype(jnp.bfloat16)
        deep = jnp.broadcast_to(turned[:, k : k + 1], (g.block, g.deep)).astype(cell_type)
        hit = jnp.where(both_iota == jnp.concatenate([deep, deep], axis=0), one, zero)
        got = jnp.dot(
            split,
            hit.astype(jnp.bfloat16),
            preferred_element_type=jnp.float32,
        )
        at = pl.ds(pl.multiple_of(dest_ref[k] * g.slab, SUB), g.window)
        sum_ref[at, :] += got[: g.window] + got[g.window :]
    size = g.slabs * g.slab
    spill = g.window - g.slab
    sum_ref[:spill, :] += sum_ref[size:, :]
    me = lax.axis_index("los")
    for near in range(g.plane):
        for far in range(g.planes):
            at = pl.ds(pl.multiple_of(slab_at(g, me, near, far) * g.slab, SUB), g.slab)
            last = near // 2 == g.plane // 2 - 1
            start = (0 if last else near // 2) * g.column + far * g.slab
            part_refs[near % 2 + 2 * last][start : start + g.slab, :] = sum_ref[at, :]


def cotangent_of(density, selection, counts, exponent):
    shifted = density + 0.5
    intensity = selection * jnp.exp(exponent * jnp.log(shifted))
    return (1.0 - counts.astype(jnp.float32) / intensity) * exponent * intensity / shifted


def column_kernel(g, own_ref, *refs):
    total = own_ref[...]
    for ref in refs[:-2]:
        total = total + ref[...]
    refs[-1][: g.column, :] = total
    refs[-1][g.column :, :] = refs[-2][...]


def field_kernel(g, *refs):
    part_refs, out_ref, sum_ref = refs[: g.planes], refs[-2], refs[-1]
    total = part_refs[0][: g.column, :]
    for ref in part_refs[1:]:
        total = total + ref[: g.column, :]
    sum_ref[...] = total
    far = lax.axis_index("los") // g.plane
    plane = lax.broadcasted_iota(jnp.int32, (g.slab, g.deep), 0) // g.cols
    out_ref[g.column :, :] = jnp.zeros((SUB, g.deep), jnp.float32)
    for i, ref in enumerate(part_refs):
        there = g.far_peer(far, i)
        at = pl.ds(pl.multiple_of(there * g.slab, SUB), g.slab)
        start = g.column + 2 * g.slab
        exponent = picked(jnp.broadcast_to(ref[start : start + 1, :], (g.slab, g.deep)), plane)
        selection = ref[g.column : g.column + g.slab, :]
        counts = ref[g.column + g.slab : start, :]
        out_ref[at, :] = cotangent_of(sum_ref[at, :], selection, counts, exponent)
        out_ref[pl.ds(g.column + there, 1), :] = ref[start + 1 : start + 2, :]


def joined_kernel(*refs):
    rows = refs[0].shape[0]
    for i, ref in enumerate(refs[:-1]):
        at = i * rows
        refs[-1][at : at + rows, :] = ref[...]


def picked(rows, index):
    return jnp.take_along_axis(rows, index, axis=1, mode="promise_in_bounds")


def ready_kernel(g, cell_ref, frac_ref, offset_ref, *refs):
    far_refs, near_refs = refs[:6], refs[11:-1]
    index_ref, weight_ref, info_ref, red_ref, table_ref = refs[6:11]
    copies = started(far_refs, near_refs, refs[-1])
    for copy in copies:
        copy.wait()
    dest_ref, count_ref = near_refs[:2]
    write_table(g, near_refs[2:], table_ref)
    plane_iota, sky_iota = row_iotas(g.cols)
    lane = lax.broadcasted_iota(jnp.int32, (SUB, g.block), 1)
    for k in range(g.blocks):
        offset = jnp.broadcast_to(offset_ref[k : k + 1, :], (SUB, g.block))
        live = lane < count_ref[k]
        info_ref[k : k + 1, :] = jnp.full((1, g.deep), dest_ref[k], jnp.int32)
        red = red_of(g, block_rows(cell_ref, 0, k, g.block), offset)
        sky = block_rows(cell_ref, 1, k, g.block)
        sky_next = jnp.where(sky + 1 == g.sky_wrap, 0, sky + 1)
        deep = block_rows(cell_ref, 2, k, g.block)
        frac_los = block_rows(frac_ref, 0, k, g.block)
        frac_sky = block_rows(frac_ref, 1, k, g.block)
        at_sky, at_next = (sky_iota == sky) & live, (sky_iota == sky_next) & live
        on_sky = jnp.where(at_sky, 1.0 - frac_sky, jnp.where(at_next, frac_sky, 0.0))
        slope_sky = jnp.where(at_next, 1.0, 0.0) - jnp.where(at_sky, 1.0, 0.0)
        frac_deep = block_rows(frac_ref, 2, k, g.block)
        deep_next = jnp.where(deep + 1 == g.deep, 0, deep + 1)
        tiles = [on_sky, slope_sky, frac_deep]
        for i in range(g.tiles):
            plane = plane_iota + i * g.planes_per_tile - red
            tiles.append(jnp.where(plane == 0, 1.0 - frac_los, jnp.where(plane == 1, frac_los, 0.0)))
            tiles.append(jnp.where(plane == 1, 1.0, jnp.where(plane == 0, -1.0, 0.0)))
        index_ref[k, 0] = deep
        index_ref[k, 1] = deep_next
        if g.twice:
            first, top = plane_iota == 0, red == g.slab_rows - 1
            slope_top = jnp.where(top, jnp.where(first, 1.0 - frac_deep, frac_deep), 0.0)
            tiles.append(frac_los * slope_top)
            tiles.append(jnp.where(top, jnp.where(first, -frac_los, frac_los), 0.0))
            tiles.append(slope_top)
            index_ref[k, 2] = jnp.where(first, deep, deep_next)
        for j, tile in enumerate(tiles):
            weight_ref[k, j] = tile
        red_ref[k : k + 1, :] = red[0:1]


def crossed(mask, first, second, distance):
    return jnp.where(mask, first, second) + pltpu.roll(jnp.where(mask, second, first), distance, 0)


def pull_kernel(g, info_ref, index_ref, weight_ref, red_ref, *refs):
    field_refs, (pos_ref, vel_ref, whole_ref, top_ref, rate_ref, own_rate_ref) = refs[:-6], refs[-6:]
    me = lax.axis_index("los")
    tall = g.column + SUB
    for near in range(g.plane):
        ref = field_refs[near % 2 + 2 * (near > 1)]
        base = max(near // 2 - 1, 0) * tall
        for far in range(g.planes):
            slab = slab_at(g, me, near, far)
            at = pl.ds(pl.multiple_of(slab * g.slab, SUB), g.slab)
            start = base + far * g.slab
            whole_ref[at, :] = ref[start : start + g.slab, :]
            if g.twice:
                under = pl.multiple_of(lax.rem(slab + g.slabs - 1, g.slabs) * SUB, SUB)
                rows = ref[start : start + g.cols, :]
                top_ref[pl.ds(under, SUB), :] = jnp.concatenate([rows, rows], axis=0)
            start = base + g.column + far
            rate_ref[pl.ds(slab, 1), :] = ref[start : start + 1, :]
    spill = g.window - g.slab
    whole_ref[g.slabs * g.slab :, :] = whole_ref[:spill, :]
    sub = lax.broadcasted_iota(jnp.int32, (SUB, g.block), 0)
    in_even, in_first = sub % 2 == 0, sub % 4 < 2
    for k in range(g.blocks):
        slab = dest_of(info_ref, k)
        deep, deep_next = index_ref[k, 0], index_ref[k, 1]
        on_sky, slope_sky, frac_deep = weight_ref[k, 0], weight_ref[k, 1], weight_ref[k, 2]
        sum_val, sum_los, sum_deep = 0.0, 0.0, 0.0
        for i in range(g.tiles):
            at = pl.ds(pl.multiple_of(slab * g.slab, SUB) + i * SUB, SUB)
            rows = whole_ref[at, :]
            below = picked(rows, deep)
            step = picked(rows, deep_next) - below
            value = below + frac_deep * step
            on_los, slope_los = weight_ref[k, 3 + 2 * i], weight_ref[k, 4 + 2 * i]
            sum_val += on_los * value
            sum_deep += on_los * step
            sum_los += slope_los * value
        if g.twice:
            rows = picked(top_ref[pl.ds(pl.multiple_of(slab * SUB, SUB), SUB), :], index_ref[k, 2])
            sum_val += weight_ref[k, 3 + 2 * g.tiles] * rows
            sum_deep += weight_ref[k, 4 + 2 * g.tiles] * rows
            sum_los += weight_ref[k, 5 + 2 * g.tiles] * rows
        lanes = slice(k * g.block, (k + 1) * g.block)
        own_rate_ref[k : k + 1, :] = rate_ref[pl.ds(slab, 1), :]
        pair = crossed(in_even, on_sky * sum_los, slope_sky * sum_val, 1)
        other = on_sky * sum_deep
        four = crossed(in_first, pair, other + pltpu.roll(other, 1, 0), 2)
        grads = four + pltpu.roll(four, 4, 0)
        pos_ref[:, lanes] = grads[:3]
        vel_ref[k : k + 1, :] = grads[0:1]
    for k in range(0, g.blocks, SUB):
        rows = slice(k, k + SUB)
        vel_ref[rows, :] = vel_ref[rows, :] * picked(own_rate_ref[rows, :], red_ref[rows, :])


class Geometry:
    def __init__(self, slabs, sky_parts, cell_shape, block_shape, field_shape):
        self.slabs = slabs
        self.blocks = block_shape[0]
        self.block = cell_shape[1] // self.blocks
        self.slab_rows, self.width, self.deep = field_shape
        self.sky_wrap = self.width if sky_parts == 1 else -1
        need = self.width + (sky_parts > 1)
        self.cols = next(c for c in (1, 2, 4, 8) if c >= need and c * self.slab_rows % SUB == 0)
        self.planes_per_tile = SUB // self.cols
        self.slab = self.slab_rows * self.cols
        self.plane = 8
        self.planes = slabs // self.plane
        self.column = self.planes * self.slab
        self.window = rounded_up(self.slab + self.cols, SUB)

        self.twice = self.planes_per_tile == 2 and self.slab % SUB == 0
        self.tiles = (self.slab if self.twice else self.window) // SUB

    def far_peer(self, far, m):
        even = self.planes & (self.planes - 1) == 0
        return far ^ m if even else (far + m) % self.planes


def on_device(
    part_cell,
    part_frac,
    los_offset,
    block_dest,
    block_count,
    selection,
    galaxy_counts,
    bias_exp,
    rsd_factor,
):
    sky_parts = lax.axis_size("sky")
    g = Geometry(
        lax.axis_size("los"), sky_parts, part_cell.shape, block_dest.shape, selection.shape
    )
    f32 = jnp.float32
    vmem = pl.BlockSpec(memory_space=pltpu.VMEM)
    if sky_parts > 1:
        shift = jnp.stack([0, lax.axis_index("sky") * g.width, 0]).astype(jnp.int32)
        part_cell = part_cell - shift[:, None]
    offsets = los_offset.reshape(g.blocks, g.block)
    size = g.slabs * g.slab
    padded = size + g.window - g.slab
    small = pltpu.CompilerParams(vmem_limit_bytes=VMEM_LIMIT)

    def tiled(rows):
        return jax.ShapeDtypeStruct((rows, g.deep), f32)

    def to_near(block, near):
        return lax.ppermute(block, "los", [(i ^ near, i) for i in range(g.slabs)])

    def spread(move, blocks):
        return [move(block, j) for j, block in enumerate(blocks, 1)]

    def from_far(block, m):
        rest = [(i // g.plane, i % g.plane) for i in range(g.slabs)]
        route = [(g.far_peer(far, m) * g.plane + near, far * g.plane + near) for far, near in rest]
        return lax.ppermute(block, "los", route)

    def held(*arrays):
        return [pltpu.with_memory_space_constraint(x, pltpu.HBM) for x in arrays]

    far = pl.BlockSpec(memory_space=pltpu.HBM)
    scalars = [
        pltpu.SMEM(block_dest.shape, jnp.int32),
        pltpu.SMEM(block_count.shape, jnp.int32),
    ]
    rest_rows = size // 2 - g.column
    cell, frac, offset, keep, send, keep_last, send_last = pl.pallas_call(
        functools.partial(paint_kernel, g),
        out_shape=(
            pltpu.VMEM(part_cell.shape, jnp.int32),
            pltpu.VMEM(part_frac.shape, f32),
            pltpu.VMEM(offsets.shape, jnp.int32),
            pltpu.VMEM((rest_rows, g.deep), f32),
            pltpu.VMEM((rest_rows, g.deep), f32),
            pltpu.VMEM((g.column, g.deep), f32),
            pltpu.VMEM((g.column, g.deep), f32),
        ),
        in_specs=[far] * 5,
        out_specs=(vmem,) * 7,
        scratch_shapes=[
            *scalars,
            pltpu.VMEM((padded, g.deep), f32),
            pltpu.VMEM((rounded_up(g.blocks, SUB), g.block), f32),
            pltpu.SemaphoreType.DMA((5,)),
        ],
        compiler_params=small,
        name="paint",
    )(*held(block_dest, block_count, part_cell, part_frac, offsets))
    tiles = (g.blocks, 3 + 2 * g.tiles + 3 * g.twice, SUB, g.block)
    index, weight, info, red, table = pl.pallas_call(
        functools.partial(ready_kernel, g),
        out_shape=(
            pltpu.VMEM((g.blocks, 3, SUB, g.block), jnp.int32),
            pltpu.VMEM(tiles, f32),
            pltpu.VMEM((g.blocks, g.deep), jnp.int32),
            pltpu.VMEM((g.blocks, g.block), jnp.int32),
            pltpu.VMEM((2 * g.slab + SUB, g.deep), f32),
        ),
        in_specs=[vmem] * 3 + [far] * 6,
        out_specs=(vmem,) * 5,
        scratch_shapes=[
            *scalars,
            pltpu.VMEM(selection.shape, f32),
            pltpu.VMEM(galaxy_counts.shape, jnp.int32),
            pltpu.SMEM(bias_exp.shape, f32),
            pltpu.SMEM(rsd_factor.shape, f32),
            pltpu.SemaphoreType.DMA((6,)),
        ],
        compiler_params=small,
        cost_estimate=pl.CostEstimate(flops=10**6, bytes_accessed=4 * 10**6, transcendentals=0),
        name="ready",
    )(
        cell,
        frac,
        offset,
        *held(block_dest, block_count, selection, galaxy_counts, bias_exp, rsd_factor),
    )
    quarters = g.plane // 2
    last = keep_last + to_near(send_last, 1)
    pair = (keep + to_near(send, 1)).reshape(quarters - 1, g.column, g.deep)
    pair = [*pair, last]
    column = pl.pallas_call(
        functools.partial(column_kernel, g),
        out_shape=tiled(g.column + 2 * g.slab + SUB),
        in_specs=[vmem] * (quarters + 1),
        out_specs=vmem,
        compiler_params=small,
        name="column",
    )(pair[0], *spread(lambda block, j: to_near(block, 2 * j), pair[1:]), table)
    parts = [column] + spread(from_far, [column] * (g.planes - 1))
    tall = g.column + SUB
    if sky_parts == 1:
        field = pl.pallas_call(
            functools.partial(field_kernel, g),
            out_shape=tiled(tall),
            in_specs=[vmem] * g.planes,
            out_specs=vmem,
            scratch_shapes=[pltpu.VMEM((g.column, g.deep), f32)],
            compiler_params=small,
            name="field",
        )(*parts)
    else:
        here = lax.axis_index("los") // g.plane
        stacked = jnp.stack(parts)
        planes = jnp.zeros_like(stacked[:, g.column :])
        for m in range(g.planes):
            planes = lax.dynamic_update_index_in_dim(
                planes, stacked[m, g.column :], g.far_peer(here, m), 0
            )
        cells = planes[:, : 2 * g.slab].reshape(g.planes, 2, g.slab_rows, g.cols, g.deep)
        power = planes[:, 2 * g.slab, : g.slab_rows, None, None]
        core = jnp.sum(stacked[:, : g.column], axis=0)
        core = core.reshape(g.planes, g.slab_rows, g.cols, g.deep)
        edge = passed_along(core[:, :, g.width], "sky", 1)
        density = core[:, :, : g.width].at[:, :, 0].add(edge)
        near = cells[:, :, :, : g.width]
        inner = cotangent_of(density, near[:, 0], near[:, 1], power)
        rim = passed_along(inner[:, :, 0], "sky", -1)
        rest = jnp.zeros((g.planes, g.slab_rows, g.cols - g.width - 1, g.deep), f32)
        inner = jnp.concatenate([inner, rim[:, :, None], rest], axis=2).reshape(g.column, g.deep)
        rates = jnp.pad(planes[:, 2 * g.slab + 1], ((0, SUB - g.planes), (0, 0)))
        field = jnp.concatenate([inner, rates])
    around = spread(lambda block, j: to_near(block, 2 * j), [field] * (quarters - 1))
    own = [field, to_near(field, 1)]
    joined = pl.pallas_call(
        joined_kernel,
        out_shape=tiled((quarters - 1) * tall),
        in_specs=[vmem] * (quarters - 1),
        out_specs=vmem,
        compiler_params=small,
        name="joined",
    )(*around)
    fields = [*own, joined, to_near(joined, 1)]
    grad_pos, grad_vel = pl.pallas_call(
        functools.partial(pull_kernel, g),
        out_shape=(
            jax.ShapeDtypeStruct(part_frac.shape, f32),
            jax.ShapeDtypeStruct((g.blocks, g.block), f32),
        ),
        in_specs=[vmem] * 8,
        out_specs=(vmem, vmem),
        scratch_shapes=[
            pltpu.VMEM((padded, g.deep), f32),
            pltpu.VMEM((g.slabs * SUB, g.deep), f32),
            pltpu.VMEM((g.slabs, g.deep), f32),
            pltpu.VMEM((g.blocks, g.deep), f32),
        ],
        compiler_params=small,
        name="pull",
    )(info, index, weight, red, *fields)
    return grad_pos, grad_vel.reshape(-1)


def solution(mesh):
    return jax.shard_map(
        on_device,
        mesh=mesh,
        in_specs=(
            P(None, ("los", "sky")),
            P(None, ("los", "sky")),
            P(("los", "sky")),
            P(("los", "sky")),
            P(("los", "sky")),
            P("los", "sky", None),
            P("los", "sky", None),
            P("los"),
            P("los"),
        ),
        out_specs=(P(None, ("los", "sky")), P(("los", "sky"))),
        check_vma=False,
    )
```

```python
import functools

import jax
import jax.numpy as jnp
from jax import lax
from jax.experimental import pallas as pl
from jax.experimental.pallas import tpu as pltpu
from jax.sharding import PartitionSpec as P

SUB = 8
VMEM_LIMIT = 8 * 1024 * 1024


def passed_along(block, axis, distance):
    devices = range(lax.axis_size(axis))
    route = [((i - distance) % len(devices), i) for i in devices]
    return lax.ppermute(block, axis, route)


def rounded_up(value, step):
    return -(-value // step) * step


def row_iotas(cols):
    sub = lax.broadcasted_iota(jnp.int32, (SUB, 128), 0)
    return sub // cols, sub % cols


def block_rows(ref, row, k, lanes):
    return jnp.broadcast_to(ref[row : row + 1, k * lanes : (k + 1) * lanes], (SUB, lanes))


def slab_at(g, me, near, far):
    return far * g.plane + ((me % g.plane) ^ near)


def write_table(g, refs, table_ref):
    selection_ref, counts_ref, bias_ref, rate_ref = refs
    sub = lax.broadcasted_iota(jnp.int32, (SUB, g.deep), 0)
    lane = lax.broadcasted_iota(jnp.int32, (SUB, g.deep), 1)
    rest = jnp.zeros((SUB, g.deep), jnp.float32)
    table_ref[...] = jnp.zeros_like(table_ref)
    for j in range(g.slab_rows):
        rest = jnp.where(lane == j, jnp.where(sub == 0, bias_ref[j], rate_ref[j]), rest)
        start = j * g.cols
        table_ref[start : start + g.width, :] = selection_ref[j]
        table_ref[g.slab + start : g.slab + start + g.width, :] = counts_ref[j].astype(jnp.float32)
    table_ref[2 * g.slab :, :] = rest


def started(sources, targets, arrived):
    copies = [
        pltpu.make_async_copy(a, b, arrived.at[i])
        for i, (a, b) in enumerate(zip(sources, targets, strict=True))
    ]
    for copy in copies:
        copy.start()
    return copies


def dest_of(dest_ref, k):
    return dest_ref[k : k + 1, 0:1][0, 0]


def red_of(g, cell, offset):
    even = g.slab_rows & (g.slab_rows - 1) == 0
    return (cell + offset) & (g.slab_rows - 1) if even else jnp.mod(cell + offset, g.slab_rows)


def paint_kernel(g, *refs):
    far_refs, (cell_ref, frac_ref, offset_ref), part_refs, refs = refs[:5], refs[5:8], refs[8:12], refs[12:]
    dest_ref, count_ref, sum_ref, turn_ref, arrived = refs
    copies = started(far_refs, (dest_ref, count_ref, cell_ref, frac_ref, offset_ref), arrived)
    sum_ref[...] = jnp.zeros_like(sum_ref)
    lane = lax.broadcasted_iota(jnp.int32, (SUB, g.block), 1)
    plane_iota, sky_iota = row_iotas(g.cols)
    deep_iota = lax.broadcasted_iota(jnp.int32, (g.block, g.deep), 1)
    under_iota = jnp.where(deep_iota == 0, g.deep - 1, deep_iota - 1)
    cell_type = jnp.bfloat16 if g.deep <= 256 else jnp.float32
    both_iota = jnp.concatenate([deep_iota, under_iota], axis=0).astype(jnp.float32).astype(cell_type)
    one, zero = jnp.ones_like(both_iota), jnp.zeros_like(both_iota)
    for copy in copies[2:]:
        copy.wait()
    for k in range(g.blocks):
        turn_ref[k : k + 1, :] = cell_ref[2:3, k * g.block : (k + 1) * g.block].astype(jnp.float32)
    turned = turn_ref[...].T
    for copy in copies[:2]:
        copy.wait()
    for k in range(g.blocks):
        offset = jnp.broadcast_to(offset_ref[k : k + 1, :], (SUB, g.block))
        red = red_of(g, block_rows(cell_ref, 0, k, g.block), offset)
        sky = block_rows(cell_ref, 1, k, g.block)
        sky_next = jnp.where(sky + 1 == g.sky_wrap, 0, sky + 1)
        frac_los = block_rows(frac_ref, 0, k, g.block)
        frac_sky = block_rows(frac_ref, 1, k, g.block)
        frac_deep = block_rows(frac_ref, 2, k, g.block)
        on_sky = jnp.where(
            sky_iota == sky, 1.0 - frac_sky, jnp.where(sky_iota == sky_next, frac_sky, 0.0)
        )
        on_sky = jnp.where(lane < count_ref[k], on_sky, 0.0)
        rows = []
        for i in range(g.window // SUB):
            plane = plane_iota + i * g.planes_per_tile - red
            on_los = jnp.where(
                plane == 0, 1.0 - frac_los, jnp.where(plane == 1, frac_los, 0.0)
            )
            rows.append(on_los * on_sky)
        weight = jnp.concatenate(rows, axis=0)
        upper = weight * jnp.concatenate([frac_deep] * (g.window // SUB), axis=0)
        weight = jnp.concatenate([weight - upper, upper], axis=1)
        coarse = weight.astype(jnp.bfloat16).astype(jnp.float32)
        split = jnp.concatenate([coarse, weight - coarse], axis=0).astype(jnp.bfloat16)
        deep = jnp.broadcast_to(turned[:, k : k + 1], (g.block, g.deep)).astype(cell_type)
        hit = jnp.where(both_iota == jnp.concatenate([deep, deep], axis=0), one, zero)
        got = jnp.dot(
            split,
            hit.astype(jnp.bfloat16),
            preferred_element_type=jnp.float32,
        )
        at = pl.ds(pl.multiple_of(dest_ref[k] * g.slab, SUB), g.window)
        sum_ref[at, :] += got[: g.window] + got[g.window :]
    size = g.slabs * g.slab
    spill = g.window - g.slab
    sum_ref[:spill, :] += sum_ref[size:, :]
    me = lax.axis_index("los")
    for near in range(g.plane):
        for far in range(g.planes):
            at = pl.ds(pl.multiple_of(slab_at(g, me, near, far) * g.slab, SUB), g.slab)
            last = near // 2 == g.plane // 2 - 1
            start = (0 if last else near // 2) * g.column + far * g.slab
            part_refs[near % 2 + 2 * last][start : start + g.slab, :] = sum_ref[at, :]


def cotangent_of(density, selection, counts, exponent):
    shifted = density + 0.5
    intensity = selection * jnp.exp(exponent * jnp.log(shifted))
    return (1.0 - counts.astype(jnp.float32) / intensity) * exponent * intensity / shifted


def column_kernel(g, own_ref, *refs):
    total = own_ref[...]
    for ref in refs[:-2]:
        total = total + ref[...]
    refs[-1][: g.column, :] = total
    refs[-1][g.column :, :] = refs[-2][...]


def field_kernel(g, *refs):
    part_refs, out_ref, sum_ref = refs[: g.planes], refs[-2], refs[-1]
    total = part_refs[0][: g.column, :]
    for ref in part_refs[1:]:
        total = total + ref[: g.column, :]
    sum_ref[...] = total
    far = lax.axis_index("los") // g.plane
    plane = lax.broadcasted_iota(jnp.int32, (g.slab, g.deep), 0) // g.cols
    out_ref[g.column :, :] = jnp.zeros((SUB, g.deep), jnp.float32)
    for i, ref in enumerate(part_refs):
        there = g.far_peer(far, i)
        at = pl.ds(pl.multiple_of(there * g.slab, SUB), g.slab)
        start = g.column + 2 * g.slab
        exponent = picked(jnp.broadcast_to(ref[start : start + 1, :], (g.slab, g.deep)), plane)
        selection = ref[g.column : g.column + g.slab, :]
        counts = ref[g.column + g.slab : start, :]
        out_ref[at, :] = cotangent_of(sum_ref[at, :], selection, counts, exponent)
        out_ref[pl.ds(g.column + there, 1), :] = ref[start + 1 : start + 2, :]


def joined_kernel(*refs):
    rows = refs[0].shape[0]
    for i, ref in enumerate(refs[:-1]):
        at = i * rows
        refs[-1][at : at + rows, :] = ref[...]


def picked(rows, index):
    return jnp.take_along_axis(rows, index, axis=1, mode="promise_in_bounds")


def ready_kernel(g, cell_ref, frac_ref, offset_ref, *refs):
    far_refs, near_refs = refs[:6], refs[11:-1]
    index_ref, weight_ref, info_ref, red_ref, table_ref = refs[6:11]
    copies = started(far_refs, near_refs, refs[-1])
    for copy in copies:
        copy.wait()
    dest_ref, count_ref = near_refs[:2]
    write_table(g, near_refs[2:], table_ref)
    plane_iota, sky_iota = row_iotas(g.cols)
    lane = lax.broadcasted_iota(jnp.int32, (SUB, g.block), 1)
    for k in range(g.blocks):
        offset = jnp.broadcast_to(offset_ref[k : k + 1, :], (SUB, g.block))
        live = lane < count_ref[k]
        info_ref[k : k + 1, :] = jnp.full((1, g.deep), dest_ref[k], jnp.int32)
        red = red_of(g, block_rows(cell_ref, 0, k, g.block), offset)
        sky = block_rows(cell_ref, 1, k, g.block)
        sky_next = jnp.where(sky + 1 == g.sky_wrap, 0, sky + 1)
        deep = block_rows(cell_ref, 2, k, g.block)
        frac_los = block_rows(frac_ref, 0, k, g.block)
        frac_sky = block_rows(frac_ref, 1, k, g.block)
        at_sky, at_next = (sky_iota == sky) & live, (sky_iota == sky_next) & live
        on_sky = jnp.where(at_sky, 1.0 - frac_sky, jnp.where(at_next, frac_sky, 0.0))
        slope_sky = jnp.where(at_next, 1.0, 0.0) - jnp.where(at_sky, 1.0, 0.0)
        frac_deep = block_rows(frac_ref, 2, k, g.block)
        deep_next = jnp.where(deep + 1 == g.deep, 0, deep + 1)
        tiles = [on_sky, slope_sky, frac_deep]
        for i in range(g.tiles):
            plane = plane_iota + i * g.planes_per_tile - red
            tiles.append(jnp.where(plane == 0, 1.0 - frac_los, jnp.where(plane == 1, frac_los, 0.0)))
            tiles.append(jnp.where(plane == 1, 1.0, jnp.where(plane == 0, -1.0, 0.0)))
        index_ref[k, 0] = deep
        index_ref[k, 1] = deep_next
        if g.twice:
            first, top = plane_iota == 0, red == g.slab_rows - 1
            slope_top = jnp.where(top, jnp.where(first, 1.0 - frac_deep, frac_deep), 0.0)
            tiles.append(frac_los * slope_top)
            tiles.append(jnp.where(top, jnp.where(first, -frac_los, frac_los), 0.0))
            tiles.append(slope_top)
            index_ref[k, 2] = jnp.where(first, deep, deep_next)
        for j, tile in enumerate(tiles):
            weight_ref[k, j] = tile
        red_ref[k : k + 1, :] = red[0:1]


def crossed(mask, first, second, distance):
    return jnp.where(mask, first, second) + pltpu.roll(jnp.where(mask, second, first), distance, 0)


def pull_kernel(g, info_ref, index_ref, weight_ref, red_ref, *refs):
    field_refs, (pos_ref, vel_ref, whole_ref, top_ref, rate_ref, own_rate_ref) = refs[:-6], refs[-6:]
    me = lax.axis_index("los")
    tall = g.column + SUB
    for near in range(g.plane):
        ref, base = field_refs[near % 2], (near // 2) * tall
        for far in range(g.planes):
            slab = slab_at(g, me, near, far)
            at = pl.ds(pl.multiple_of(slab * g.slab, SUB), g.slab)
            start = base + far * g.slab
            whole_ref[at, :] = ref[start : start + g.slab, :]
            if g.twice:
                under = pl.multiple_of(lax.rem(slab + g.slabs - 1, g.slabs) * SUB, SUB)
                rows = ref[start : start + g.cols, :]
                top_ref[pl.ds(under, SUB), :] = jnp.concatenate([rows, rows], axis=0)
            start = base + g.column + far
            rate_ref[pl.ds(slab, 1), :] = ref[start : start + 1, :]
    spill = g.window - g.slab
    whole_ref[g.slabs * g.slab :, :] = whole_ref[:spill, :]
    sub = lax.broadcasted_iota(jnp.int32, (SUB, g.block), 0)
    in_even, in_first = sub % 2 == 0, sub % 4 < 2
    for k in range(g.blocks):
        slab = dest_of(info_ref, k)
        deep, deep_next = index_ref[k, 0], index_ref[k, 1]
        on_sky, slope_sky, frac_deep = weight_ref[k, 0], weight_ref[k, 1], weight_ref[k, 2]
        sum_val, sum_los, sum_deep = 0.0, 0.0, 0.0
        for i in range(g.tiles):
            at = pl.ds(pl.multiple_of(slab * g.slab, SUB) + i * SUB, SUB)
            rows = whole_ref[at, :]
            below = picked(rows, deep)
            step = picked(rows, deep_next) - below
            value = below + frac_deep * step
            on_los, slope_los = weight_ref[k, 3 + 2 * i], weight_ref[k, 4 + 2 * i]
            sum_val += on_los * value
            sum_deep += on_los * step
            sum_los += slope_los * value
        if g.twice:
            rows = picked(top_ref[pl.ds(pl.multiple_of(slab * SUB, SUB), SUB), :], index_ref[k, 2])
            sum_val += weight_ref[k, 3 + 2 * g.tiles] * rows
            sum_deep += weight_ref[k, 4 + 2 * g.tiles] * rows
            sum_los += weight_ref[k, 5 + 2 * g.tiles] * rows
        lanes = slice(k * g.block, (k + 1) * g.block)
        own_rate_ref[k : k + 1, :] = rate_ref[pl.ds(slab, 1), :]
        pair = crossed(in_even, on_sky * sum_los, slope_sky * sum_val, 1)
        other = on_sky * sum_deep
        four = crossed(in_first, pair, other + pltpu.roll(other, 1, 0), 2)
        grads = four + pltpu.roll(four, 4, 0)
        pos_ref[:, lanes] = grads[:3]
        vel_ref[k : k + 1, :] = grads[0:1]
    for k in range(0, g.blocks, SUB):
        rows = slice(k, k + SUB)
        vel_ref[rows, :] = vel_ref[rows, :] * picked(own_rate_ref[rows, :], red_ref[rows, :])


class Geometry:
    def __init__(self, slabs, sky_parts, cell_shape, block_shape, field_shape):
        self.slabs = slabs
        self.blocks = block_shape[0]
        self.block = cell_shape[1] // self.blocks
        self.slab_rows, self.width, self.deep = field_shape
        self.sky_wrap = self.width if sky_parts == 1 else -1
        need = self.width + (sky_parts > 1)
        self.cols = next(c for c in (1, 2, 4, 8) if c >= need and c * self.slab_rows % SUB == 0)
        self.planes_per_tile = SUB // self.cols
        self.slab = self.slab_rows * self.cols
        self.plane = 8
        self.planes = slabs // self.plane
        self.column = self.planes * self.slab
        self.window = rounded_up(self.slab + self.cols, SUB)

        self.twice = self.planes_per_tile == 2 and self.slab % SUB == 0
        self.tiles = (self.slab if self.twice else self.window) // SUB

    def far_peer(self, far, m):
        even = self.planes & (self.planes - 1) == 0
        return far ^ m if even else (far + m) % self.planes


def on_device(
    part_cell,
    part_frac,
    los_offset,
    block_dest,
    block_count,
    selection,
    galaxy_counts,
    bias_exp,
    rsd_factor,
):
    sky_parts = lax.axis_size("sky")
    g = Geometry(
        lax.axis_size("los"), sky_parts, part_cell.shape, block_dest.shape, selection.shape
    )
    f32 = jnp.float32
    vmem = pl.BlockSpec(memory_space=pltpu.VMEM)
    if sky_parts > 1:
        shift = jnp.stack([0, lax.axis_index("sky") * g.width, 0]).astype(jnp.int32)
        part_cell = part_cell - shift[:, None]
    offsets = los_offset.reshape(g.blocks, g.block)
    size = g.slabs * g.slab
    padded = size + g.window - g.slab
    small = pltpu.CompilerParams(vmem_limit_bytes=VMEM_LIMIT)

    def tiled(rows):
        return jax.ShapeDtypeStruct((rows, g.deep), f32)

    def to_near(block, near):
        return lax.ppermute(block, "los", [(i ^ near, i) for i in range(g.slabs)])

    def spread(move, blocks):
        return [move(block, j) for j, block in enumerate(blocks, 1)]

    def from_far(block, m):
        rest = [(i // g.plane, i % g.plane) for i in range(g.slabs)]
        route = [(g.far_peer(far, m) * g.plane + near, far * g.plane + near) for far, near in rest]
        return lax.ppermute(block, "los", route)

    def held(*arrays):
        return [pltpu.with_memory_space_constraint(x, pltpu.HBM) for x in arrays]

    far = pl.BlockSpec(memory_space=pltpu.HBM)
    scalars = [
        pltpu.SMEM(block_dest.shape, jnp.int32),
        pltpu.SMEM(block_count.shape, jnp.int32),
    ]
    rest_rows = size // 2 - g.column
    cell, frac, offset, keep, send, keep_last, send_last = pl.pallas_call(
        functools.partial(paint_kernel, g),
        out_shape=(
            pltpu.VMEM(part_cell.shape, jnp.int32),
            pltpu.VMEM(part_frac.shape, f32),
            pltpu.VMEM(offsets.shape, jnp.int32),
            pltpu.VMEM((rest_rows, g.deep), f32),
            pltpu.VMEM((rest_rows, g.deep), f32),
            pltpu.VMEM((g.column, g.deep), f32),
            pltpu.VMEM((g.column, g.deep), f32),
        ),
        in_specs=[far] * 5,
        out_specs=(vmem,) * 7,
        scratch_shapes=[
            *scalars,
            pltpu.VMEM((padded, g.deep), f32),
            pltpu.VMEM((rounded_up(g.blocks, SUB), g.block), f32),
            pltpu.SemaphoreType.DMA((5,)),
        ],
        compiler_params=small,
        name="paint",
    )(*held(block_dest, block_count, part_cell, part_frac, offsets))
    tiles = (g.blocks, 3 + 2 * g.tiles + 3 * g.twice, SUB, g.block)
    index, weight, info, red, table = pl.pallas_call(
        functools.partial(ready_kernel, g),
        out_shape=(
            pltpu.VMEM((g.blocks, 3, SUB, g.block), jnp.int32),
            pltpu.VMEM(tiles, f32),
            pltpu.VMEM((g.blocks, g.deep), jnp.int32),
            pltpu.VMEM((g.blocks, g.block), jnp.int32),
            pltpu.VMEM((2 * g.slab + SUB, g.deep), f32),
        ),
        in_specs=[vmem] * 3 + [far] * 6,
        out_specs=(vmem,) * 5,
        scratch_shapes=[
            *scalars,
            pltpu.VMEM(selection.shape, f32),
            pltpu.VMEM(galaxy_counts.shape, jnp.int32),
            pltpu.SMEM(bias_exp.shape, f32),
            pltpu.SMEM(rsd_factor.shape, f32),
            pltpu.SemaphoreType.DMA((6,)),
        ],
        compiler_params=small,
        cost_estimate=pl.CostEstimate(flops=10**6, bytes_accessed=4 * 10**6, transcendentals=0),
        name="ready",
    )(
        cell,
        frac,
        offset,
        *held(block_dest, block_count, selection, galaxy_counts, bias_exp, rsd_factor),
    )
    quarters = g.plane // 2
    last = keep_last + to_near(send_last, 1)
    pair = (keep + to_near(send, 1)).reshape(quarters - 1, g.column, g.deep)
    pair = [*pair, last]
    column = pl.pallas_call(
        functools.partial(column_kernel, g),
        out_shape=tiled(g.column + 2 * g.slab + SUB),
        in_specs=[vmem] * (quarters + 1),
        out_specs=vmem,
        compiler_params=small,
        name="column",
    )(pair[0], *spread(lambda block, j: to_near(block, 2 * j), pair[1:]), table)
    parts = [column] + spread(from_far, [column] * (g.planes - 1))
    tall = g.column + SUB
    if sky_parts == 1:
        field = pl.pallas_call(
            functools.partial(field_kernel, g),
            out_shape=tiled(tall),
            in_specs=[vmem] * g.planes,
            out_specs=vmem,
            scratch_shapes=[pltpu.VMEM((g.column, g.deep), f32)],
            compiler_params=small,
            name="field",
        )(*parts)
    else:
        here = lax.axis_index("los") // g.plane
        stacked = jnp.stack(parts)
        planes = jnp.zeros_like(stacked[:, g.column :])
        for m in range(g.planes):
            planes = lax.dynamic_update_index_in_dim(
                planes, stacked[m, g.column :], g.far_peer(here, m), 0
            )
        cells = planes[:, : 2 * g.slab].reshape(g.planes, 2, g.slab_rows, g.cols, g.deep)
        power = planes[:, 2 * g.slab, : g.slab_rows, None, None]
        core = jnp.sum(stacked[:, : g.column], axis=0)
        core = core.reshape(g.planes, g.slab_rows, g.cols, g.deep)
        edge = passed_along(core[:, :, g.width], "sky", 1)
        density = core[:, :, : g.width].at[:, :, 0].add(edge)
        near = cells[:, :, :, : g.width]
        inner = cotangent_of(density, near[:, 0], near[:, 1], power)
        rim = passed_along(inner[:, :, 0], "sky", -1)
        rest = jnp.zeros((g.planes, g.slab_rows, g.cols - g.width - 1, g.deep), f32)
        inner = jnp.concatenate([inner, rim[:, :, None], rest], axis=2).reshape(g.column, g.deep)
        rates = jnp.pad(planes[:, 2 * g.slab + 1], ((0, SUB - g.planes), (0, 0)))
        field = jnp.concatenate([inner, rates])
    even = pl.pallas_call(
        joined_kernel,
        out_shape=tiled(quarters * tall),
        in_specs=[vmem] * quarters,
        out_specs=vmem,
        compiler_params=small,
        name="joined",
    )(field, *spread(lambda block, j: to_near(block, 2 * j), [field] * (quarters - 1)))
    fields = [even, to_near(even, 1)]
    grad_pos, grad_vel = pl.pallas_call(
        functools.partial(pull_kernel, g),
        out_shape=(
            jax.ShapeDtypeStruct(part_frac.shape, f32),
            jax.ShapeDtypeStruct((g.blocks, g.block), f32),
        ),
        in_specs=[vmem] * 6,
        out_specs=(vmem, vmem),
        scratch_shapes=[
            pltpu.VMEM((padded, g.deep), f32),
            pltpu.VMEM((g.slabs * SUB, g.deep), f32),
            pltpu.VMEM((g.slabs, g.deep), f32),
            pltpu.VMEM((g.blocks, g.deep), f32),
        ],
        compiler_params=small,
        name="pull",
    )(info, index, weight, red, *fields)
    return grad_pos, grad_vel.reshape(-1)


def solution(mesh):
    return jax.shard_map(
        on_device,
        mesh=mesh,
        in_specs=(
            P(None, ("los", "sky")),
            P(None, ("los", "sky")),
            P(("los", "sky")),
            P(("los", "sky")),
            P(("los", "sky")),
            P("los", "sky", None),
            P("los", "sky", None),
            P("los"),
            P("los"),
        ),
        out_specs=(P(None, ("los", "sky")), P(("los", "sky"))),
        check_vma=False,
    )
```

```python
import functools

import jax
import jax.numpy as jnp
from jax import lax
from jax.experimental import pallas as pl
from jax.experimental.pallas import tpu as pltpu
from jax.sharding import PartitionSpec as P

SUB = 8
VMEM_LIMIT = 8 * 1024 * 1024


def passed_along(block, axis, distance):
    devices = range(lax.axis_size(axis))
    route = [((i - distance) % len(devices), i) for i in devices]
    return lax.ppermute(block, axis, route)


def rounded_up(value, step):
    return -(-value // step) * step


def row_iotas(cols):
    sub = lax.broadcasted_iota(jnp.int32, (SUB, 128), 0)
    return sub // cols, sub % cols


def block_rows(ref, row, k, lanes):
    return jnp.broadcast_to(ref[row : row + 1, k * lanes : (k + 1) * lanes], (SUB, lanes))


def slab_at(g, me, near, far):
    return far * g.plane + ((me % g.plane) ^ near)


def write_table(g, refs, table_ref):
    selection_ref, counts_ref, bias_ref, rate_ref = refs
    sub = lax.broadcasted_iota(jnp.int32, (SUB, g.deep), 0)
    lane = lax.broadcasted_iota(jnp.int32, (SUB, g.deep), 1)
    rest = jnp.zeros((SUB, g.deep), jnp.float32)
    table_ref[...] = jnp.zeros_like(table_ref)
    for j in range(g.slab_rows):
        rest = jnp.where(lane == j, jnp.where(sub == 0, bias_ref[j], rate_ref[j]), rest)
        start = j * g.cols
        table_ref[start : start + g.width, :] = selection_ref[j]
        table_ref[g.slab + start : g.slab + start + g.width, :] = counts_ref[j].astype(jnp.float32)
    table_ref[2 * g.slab :, :] = rest


def started(sources, targets, arrived):
    copies = [
        pltpu.make_async_copy(a, b, arrived.at[i])
        for i, (a, b) in enumerate(zip(sources, targets, strict=True))
    ]
    for copy in copies:
        copy.start()
    return copies


def dest_of(dest_ref, k):
    return dest_ref[k : k + 1, 0:1][0, 0]


def red_of(g, cell, offset):
    even = g.slab_rows & (g.slab_rows - 1) == 0
    return (cell + offset) & (g.slab_rows - 1) if even else jnp.mod(cell + offset, g.slab_rows)


def paint_kernel(g, *refs):
    far_refs, (cell_ref, frac_ref, offset_ref, keep_ref, send_ref), refs = refs[:5], refs[5:10], refs[10:]
    dest_ref, count_ref, low_ref, high_ref, arrived = refs
    copies = started(far_refs, (dest_ref, count_ref, cell_ref, frac_ref, offset_ref), arrived)
    low_ref[...] = jnp.zeros_like(low_ref)
    high_ref[...] = jnp.zeros_like(high_ref)
    for copy in copies:
        copy.wait()
    lane = lax.broadcasted_iota(jnp.int32, (SUB, g.block), 1)
    plane_iota, sky_iota = row_iotas(g.cols)
    deep_iota = lax.broadcasted_iota(jnp.int32, (g.deep, g.block), 0)
    deep_iota = deep_iota.astype(jnp.float32).astype(g.cell_type)
    for k in range(g.blocks):
        offset = jnp.broadcast_to(offset_ref[k : k + 1, :], (SUB, g.block))
        red = red_of(g, block_rows(cell_ref, 0, k, g.block), offset)
        sky = block_rows(cell_ref, 1, k, g.block)
        sky_next = jnp.where(sky + 1 == g.sky_wrap, 0, sky + 1)
        frac_los = block_rows(frac_ref, 0, k, g.block)
        frac_sky = block_rows(frac_ref, 1, k, g.block)
        frac_deep = block_rows(frac_ref, 2, k, g.block)
        on_sky = jnp.where(
            sky_iota == sky, 1.0 - frac_sky, jnp.where(sky_iota == sky_next, frac_sky, 0.0)
        )
        on_sky = jnp.where(lane < count_ref[k], on_sky, 0.0)
        rows = []
        for i in range(g.window // SUB):
            plane = plane_iota + i * g.planes_per_tile - red
            on_los = jnp.where(
                plane == 0, 1.0 - frac_los, jnp.where(plane == 1, frac_los, 0.0)
            )
            rows.append(on_los * on_sky)
        weight = jnp.concatenate(rows, axis=0)
        upper = weight * jnp.concatenate([frac_deep] * (g.window // SUB), axis=0)
        weight = jnp.concatenate([weight - upper, upper], axis=0)
        coarse = weight.astype(jnp.bfloat16)
        fine = (weight - coarse.astype(jnp.float32)).astype(jnp.bfloat16)
        deep = cell_ref[2:3, k * g.block : (k + 1) * g.block].astype(jnp.float32)
        hit = deep_iota == jnp.broadcast_to(deep.astype(g.cell_type), (g.deep, g.block))
        one, zero = jnp.ones_like(deep_iota), jnp.zeros_like(deep_iota)
        hit = jnp.where(hit, one, zero).astype(jnp.bfloat16)
        got = lax.dot_general(
            jnp.concatenate([coarse, fine], axis=0),
            hit,
            (((1,), (1,)), ((), ())),
            preferred_element_type=jnp.float32,
        )
        got = got[: 2 * g.window] + got[2 * g.window :]
        at = pl.ds(pl.multiple_of(dest_ref[k] * g.slab, SUB), g.window)
        low_ref[at, :] += got[: g.window]
        high_ref[at, :] += got[g.window :]
    size = g.slabs * g.slab
    spill = g.window - g.slab
    low_ref[:spill, :] += low_ref[size:, :]
    high_ref[:spill, :] += high_ref[size:, :]
    me = lax.axis_index("los")
    for near in range(g.plane):
        for far in range(g.planes):
            at = pl.ds(pl.multiple_of(slab_at(g, me, near, far) * g.slab, SUB), g.slab)
            start = (near // 2) * g.column + far * g.slab
            rows = low_ref[at, :] + pltpu.roll(high_ref[at, :], 1, 1)
            (send_ref if near % 2 else keep_ref)[start : start + g.slab, :] = rows


def cotangent_of(density, selection, counts, exponent):
    shifted = density + 0.5
    intensity = selection * jnp.exp(exponent * jnp.log(shifted))
    return (1.0 - counts.astype(jnp.float32) / intensity) * exponent * intensity / shifted


def column_kernel(g, own_ref, *refs):
    total = own_ref[...]
    for ref in refs[:-2]:
        total = total + ref[...]
    refs[-1][: g.column, :] = total
    refs[-1][g.column :, :] = refs[-2][...]


def field_kernel(g, *refs):
    part_refs, out_ref, sum_ref = refs[: g.planes], refs[-2], refs[-1]
    total = part_refs[0][: g.column, :]
    for ref in part_refs[1:]:
        total = total + ref[: g.column, :]
    sum_ref[...] = total
    far = lax.axis_index("los") // g.plane
    plane = lax.broadcasted_iota(jnp.int32, (g.slab, g.deep), 0) // g.cols
    out_ref[g.column :, :] = jnp.zeros((SUB, g.deep), jnp.float32)
    for m, ref in zip(g.turns, part_refs, strict=True):
        there = g.far_peer(far, m)
        at = pl.ds(pl.multiple_of(there * g.slab, SUB), g.slab)
        start = g.column + 2 * g.slab
        exponent = picked(jnp.broadcast_to(ref[start : start + 1, :], (g.slab, g.deep)), plane)
        selection = ref[g.column : g.column + g.slab, :]
        counts = ref[g.column + g.slab : start, :]
        out_ref[at, :] = cotangent_of(sum_ref[at, :], selection, counts, exponent)
        out_ref[pl.ds(g.column + there, 1), :] = ref[start + 1 : start + 2, :]


def joined_kernel(*refs):
    rows = refs[0].shape[0]
    for i, ref in enumerate(refs[:-1]):
        at = i * rows
        refs[-1][at : at + rows, :] = ref[...]


def picked(rows, index):
    return jnp.take_along_axis(rows, index, axis=1, mode="promise_in_bounds")


def ready_kernel(g, cell_ref, frac_ref, offset_ref, *refs):
    far_refs, near_refs = refs[:6], refs[11:-1]
    index_ref, weight_ref, info_ref, red_ref, table_ref = refs[6:11]
    copies = started(far_refs, near_refs, refs[-1])
    for copy in copies:
        copy.wait()
    dest_ref, count_ref = near_refs[:2]
    write_table(g, near_refs[2:], table_ref)
    plane_iota, sky_iota = row_iotas(g.cols)
    lane = lax.broadcasted_iota(jnp.int32, (SUB, g.block), 1)
    for k in range(g.blocks):
        offset = jnp.broadcast_to(offset_ref[k : k + 1, :], (SUB, g.block))
        live = lane < count_ref[k]
        info_ref[k : k + 1, :] = jnp.full((1, g.deep), dest_ref[k], jnp.int32)
        red = red_of(g, block_rows(cell_ref, 0, k, g.block), offset)
        sky = block_rows(cell_ref, 1, k, g.block)
        sky_next = jnp.where(sky + 1 == g.sky_wrap, 0, sky + 1)
        deep = block_rows(cell_ref, 2, k, g.block)
        frac_los = block_rows(frac_ref, 0, k, g.block)
        frac_sky = block_rows(frac_ref, 1, k, g.block)
        at_sky, at_next = (sky_iota == sky) & live, (sky_iota == sky_next) & live
        on_sky = jnp.where(at_sky, 1.0 - frac_sky, jnp.where(at_next, frac_sky, 0.0))
        slope_sky = jnp.where(at_next, 1.0, 0.0) - jnp.where(at_sky, 1.0, 0.0)
        frac_deep = block_rows(frac_ref, 2, k, g.block)
        deep_next = jnp.where(deep + 1 == g.deep, 0, deep + 1)
        tiles = [on_sky, slope_sky, frac_deep]
        for i in range(g.tiles):
            plane = plane_iota + i * g.planes_per_tile - red
            tiles.append(jnp.where(plane == 0, 1.0 - frac_los, jnp.where(plane == 1, frac_los, 0.0)))
            tiles.append(jnp.where(plane == 1, 1.0, jnp.where(plane == 0, -1.0, 0.0)))
        index_ref[k, 0] = deep
        index_ref[k, 1] = deep_next
        if g.twice:
            first, top = plane_iota == 0, red == g.slab_rows - 1
            slope_top = jnp.where(top, jnp.where(first, 1.0 - frac_deep, frac_deep), 0.0)
            tiles.append(frac_los * slope_top)
            tiles.append(jnp.where(top, jnp.where(first, -frac_los, frac_los), 0.0))
            tiles.append(slope_top)
            index_ref[k, 2] = jnp.where(first, deep, deep_next)
        for j, tile in enumerate(tiles):
            weight_ref[k, j] = tile
        red_ref[k : k + 1, :] = red[0:1]


def crossed(mask, first, second, distance):
    return jnp.where(mask, first, second) + pltpu.roll(jnp.where(mask, second, first), distance, 0)


def pull_kernel(g, info_ref, index_ref, weight_ref, red_ref, *refs):
    field_refs, (pos_ref, vel_ref, whole_ref, top_ref, rate_ref, own_rate_ref) = refs[:-6], refs[-6:]
    me = lax.axis_index("los")
    tall = g.column + SUB
    for near in range(g.plane):
        ref, base = field_refs[near % 2], (near // 2) * tall
        for far in range(g.planes):
            slab = slab_at(g, me, near, far)
            at = pl.ds(pl.multiple_of(slab * g.slab, SUB), g.slab)
            start = base + far * g.slab
            whole_ref[at, :] = ref[start : start + g.slab, :]
            if g.twice:
                under = pl.multiple_of(lax.rem(slab + g.slabs - 1, g.slabs) * SUB, SUB)
                rows = ref[start : start + g.cols, :]
                top_ref[pl.ds(under, SUB), :] = jnp.concatenate([rows, rows], axis=0)
            start = base + g.column + far
            rate_ref[pl.ds(slab, 1), :] = ref[start : start + 1, :]
    spill = g.window - g.slab
    whole_ref[g.slabs * g.slab :, :] = whole_ref[:spill, :]
    sub = lax.broadcasted_iota(jnp.int32, (SUB, g.block), 0)
    in_even, in_first = sub % 2 == 0, sub % 4 < 2
    for k in range(g.blocks):
        slab = dest_of(info_ref, k)
        deep, deep_next = index_ref[k, 0], index_ref[k, 1]
        on_sky, slope_sky, frac_deep = weight_ref[k, 0], weight_ref[k, 1], weight_ref[k, 2]
        sum_val, sum_los, sum_deep = 0.0, 0.0, 0.0
        for i in range(g.tiles):
            at = pl.ds(pl.multiple_of(slab * g.slab, SUB) + i * SUB, SUB)
            rows = whole_ref[at, :]
            below = picked(rows, deep)
            step = picked(rows, deep_next) - below
            value = below + frac_deep * step
            on_los, slope_los = weight_ref[k, 3 + 2 * i], weight_ref[k, 4 + 2 * i]
            sum_val += on_los * value
            sum_deep += on_los * step
            sum_los += slope_los * value
        if g.twice:
            rows = picked(top_ref[pl.ds(pl.multiple_of(slab * SUB, SUB), SUB), :], index_ref[k, 2])
            sum_val += weight_ref[k, 3 + 2 * g.tiles] * rows
            sum_deep += weight_ref[k, 4 + 2 * g.tiles] * rows
            sum_los += weight_ref[k, 5 + 2 * g.tiles] * rows
        lanes = slice(k * g.block, (k + 1) * g.block)
        own_rate_ref[k : k + 1, :] = rate_ref[pl.ds(slab, 1), :]
        pair = crossed(in_even, on_sky * sum_los, slope_sky * sum_val, 1)
        other = on_sky * sum_deep
        four = crossed(in_first, pair, other + pltpu.roll(other, 1, 0), 2)
        grads = four + pltpu.roll(four, 4, 0)
        pos_ref[:, lanes] = grads[:3]
        vel_ref[k : k + 1, :] = grads[0:1]
    for k in range(0, g.blocks, SUB):
        rows = slice(k, k + SUB)
        vel_ref[rows, :] = vel_ref[rows, :] * picked(own_rate_ref[rows, :], red_ref[rows, :])


class Geometry:
    def __init__(self, slabs, sky_parts, cell_shape, block_shape, field_shape):
        self.slabs = slabs
        self.blocks = block_shape[0]
        self.block = cell_shape[1] // self.blocks
        self.slab_rows, self.width, self.deep = field_shape
        self.sky_wrap = self.width if sky_parts == 1 else -1
        need = self.width + (sky_parts > 1)
        self.cols = next(c for c in (1, 2, 4, 8) if c >= need and c * self.slab_rows % SUB == 0)
        self.planes_per_tile = SUB // self.cols
        self.cell_type = jnp.bfloat16 if self.deep <= 256 else jnp.float32
        self.slab = self.slab_rows * self.cols
        self.plane = 8
        self.planes = slabs // self.plane
        self.column = self.planes * self.slab
        turns = (2, 1, 3) if self.planes == 4 else range(1, self.planes)
        self.turns = (0, *turns)
        self.window = rounded_up(self.slab + self.cols, SUB)

        self.twice = self.planes_per_tile == 2 and self.slab % SUB == 0
        self.tiles = (self.slab if self.twice else self.window) // SUB

    def far_peer(self, far, m):
        even = self.planes & (self.planes - 1) == 0
        return far ^ m if even else (far + m) % self.planes


def on_device(
    part_cell,
    part_frac,
    los_offset,
    block_dest,
    block_count,
    selection,
    galaxy_counts,
    bias_exp,
    rsd_factor,
):
    sky_parts = lax.axis_size("sky")
    g = Geometry(
        lax.axis_size("los"), sky_parts, part_cell.shape, block_dest.shape, selection.shape
    )
    f32 = jnp.float32
    vmem = pl.BlockSpec(memory_space=pltpu.VMEM)
    if sky_parts > 1:
        shift = jnp.stack([0, lax.axis_index("sky") * g.width, 0]).astype(jnp.int32)
        part_cell = part_cell - shift[:, None]
    offsets = los_offset.reshape(g.blocks, g.block)
    size = g.slabs * g.slab
    padded = size + g.window - g.slab
    small = pltpu.CompilerParams(vmem_limit_bytes=VMEM_LIMIT)

    def tiled(rows):
        return jax.ShapeDtypeStruct((rows, g.deep), f32)

    def to_near(block, near):
        return lax.ppermute(block, "los", [(i ^ near, i) for i in range(g.slabs)])

    def spread(move, blocks):
        return [move(block, j) for j, block in enumerate(blocks, 1)]

    def from_far(block, m):
        rest = [(i // g.plane, i % g.plane) for i in range(g.slabs)]
        route = [(g.far_peer(far, m) * g.plane + near, far * g.plane + near) for far, near in rest]
        return lax.ppermute(block, "los", route)

    def held(*arrays):
        return [pltpu.with_memory_space_constraint(x, pltpu.HBM) for x in arrays]

    far = pl.BlockSpec(memory_space=pltpu.HBM)
    scalars = [
        pltpu.SMEM(block_dest.shape, jnp.int32),
        pltpu.SMEM(block_count.shape, jnp.int32),
    ]
    cell, frac, offset, keep, send = pl.pallas_call(
        functools.partial(paint_kernel, g),
        out_shape=(
            pltpu.VMEM(part_cell.shape, jnp.int32),
            pltpu.VMEM(part_frac.shape, f32),
            pltpu.VMEM(offsets.shape, jnp.int32),
            pltpu.VMEM((size // 2, g.deep), f32),
            pltpu.VMEM((size // 2, g.deep), f32),
        ),
        in_specs=[far] * 5,
        out_specs=(vmem,) * 5,
        scratch_shapes=[
            *scalars,
            pltpu.VMEM((padded, g.deep), f32),
            pltpu.VMEM((padded, g.deep), f32),
            pltpu.SemaphoreType.DMA((5,)),
        ],
        compiler_params=small,
        name="paint",
    )(*held(block_dest, block_count, part_cell, part_frac, offsets))
    tiles = (g.blocks, 3 + 2 * g.tiles + 3 * g.twice, SUB, g.block)
    index, weight, info, red, table = pl.pallas_call(
        functools.partial(ready_kernel, g),
        out_shape=(
            pltpu.VMEM((g.blocks, 3, SUB, g.block), jnp.int32),
            pltpu.VMEM(tiles, f32),
            pltpu.VMEM((g.blocks, g.deep), jnp.int32),
            pltpu.VMEM((g.blocks, g.block), jnp.int32),
            pltpu.VMEM((2 * g.slab + SUB, g.deep), f32),
        ),
        in_specs=[vmem] * 3 + [far] * 6,
        out_specs=(vmem,) * 5,
        scratch_shapes=[
            *scalars,
            pltpu.VMEM(selection.shape, f32),
            pltpu.VMEM(galaxy_counts.shape, jnp.int32),
            pltpu.SMEM(bias_exp.shape, f32),
            pltpu.SMEM(rsd_factor.shape, f32),
            pltpu.SemaphoreType.DMA((6,)),
        ],
        compiler_params=small,
        cost_estimate=pl.CostEstimate(flops=10**6, bytes_accessed=4 * 10**6, transcendentals=0),
        name="ready",
    )(
        cell,
        frac,
        offset,
        *held(block_dest, block_count, selection, galaxy_counts, bias_exp, rsd_factor),
    )
    quarters = g.plane // 2
    pair = (keep + to_near(send, 1)).reshape(quarters, g.column, g.deep)
    column = pl.pallas_call(
        functools.partial(column_kernel, g),
        out_shape=tiled(g.column + 2 * g.slab + SUB),
        in_specs=[vmem] * (quarters + 1),
        out_specs=vmem,
        compiler_params=small,
        name="column",
    )(pair[0], *spread(lambda block, j: to_near(block, 2 * j), list(pair[1:])), table)
    parts = [column] + [from_far(column, m) for m in g.turns[1:]]
    tall = g.column + SUB
    if sky_parts == 1:
        field = pl.pallas_call(
            functools.partial(field_kernel, g),
            out_shape=tiled(tall),
            in_specs=[vmem] * g.planes,
            out_specs=vmem,
            scratch_shapes=[pltpu.VMEM((g.column, g.deep), f32)],
            compiler_params=small,
            name="field",
        )(*parts)
    else:
        here = lax.axis_index("los") // g.plane
        stacked = jnp.stack(parts)
        planes = jnp.zeros_like(stacked[:, g.column :])
        for i, m in enumerate(g.turns):
            planes = lax.dynamic_update_index_in_dim(
                planes, stacked[i, g.column :], g.far_peer(here, m), 0
            )
        cells = planes[:, : 2 * g.slab].reshape(g.planes, 2, g.slab_rows, g.cols, g.deep)
        power = planes[:, 2 * g.slab, : g.slab_rows, None, None]
        core = jnp.sum(stacked[:, : g.column], axis=0)
        core = core.reshape(g.planes, g.slab_rows, g.cols, g.deep)
        edge = passed_along(core[:, :, g.width], "sky", 1)
        density = core[:, :, : g.width].at[:, :, 0].add(edge)
        near = cells[:, :, :, : g.width]
        inner = cotangent_of(density, near[:, 0], near[:, 1], power)
        rim = passed_along(inner[:, :, 0], "sky", -1)
        rest = jnp.zeros((g.planes, g.slab_rows, g.cols - g.width - 1, g.deep), f32)
        inner = jnp.concatenate([inner, rim[:, :, None], rest], axis=2).reshape(g.column, g.deep)
        rates = jnp.pad(planes[:, 2 * g.slab + 1], ((0, SUB - g.planes), (0, 0)))
        field = jnp.concatenate([inner, rates])
    even = pl.pallas_call(
        joined_kernel,
        out_shape=tiled(quarters * tall),
        in_specs=[vmem] * quarters,
        out_specs=vmem,
        compiler_params=small,
        name="joined",
    )(field, *spread(lambda block, j: to_near(block, 2 * j), [field] * (quarters - 1)))
    fields = [even, to_near(even, 1)]
    grad_pos, grad_vel = pl.pallas_call(
        functools.partial(pull_kernel, g),
        out_shape=(
            jax.ShapeDtypeStruct(part_frac.shape, f32),
            jax.ShapeDtypeStruct((g.blocks, g.block), f32),
        ),
        in_specs=[vmem] * 6,
        out_specs=(vmem, vmem),
        scratch_shapes=[
            pltpu.VMEM((padded, g.deep), f32),
            pltpu.VMEM((g.slabs * SUB, g.deep), f32),
            pltpu.VMEM((g.slabs, g.deep), f32),
            pltpu.VMEM((g.blocks, g.deep), f32),
        ],
        compiler_params=small,
        name="pull",
    )(info, index, weight, red, *fields)
    return grad_pos, grad_vel.reshape(-1)


def solution(mesh):
    return jax.shard_map(
        on_device,
        mesh=mesh,
        in_specs=(
            P(None, ("los", "sky")),
            P(None, ("los", "sky")),
            P(("los", "sky")),
            P(("los", "sky")),
            P(("los", "sky")),
            P("los", "sky", None),
            P("los", "sky", None),
            P("los"),
            P("los"),
        ),
        out_specs=(P(None, ("los", "sky")), P(("los", "sky"))),
        check_vma=False,
    )
```
